256 devices in a mesh: row: 8 (over z_hi, y), col: 32 (over z_lo, x, core).
Axes of the slice: x: 4, y: 4, z: 8 (z_hi: 2, z_lo: 4; z = z_hi * 4 + z_lo), core: 2. Of those that a mesh axis runs over, the one named last changes fastest.
Arguments:
- fields: float32 [5, 32, 512, 1024], P(None, None, 'col', 'row'), may hold values from -1.5 to 2, as said below
Outputs:
- advanced: float32 [5, 32, 512, 1024], P(None, None, 'col', 'row')
The draws below stay inside these ranges and needn't reach their ends.
Inputs may be any that keep to these rules, and one draw needn't show every extreme that they name: `fields`: density lies in 0.5 to 2, pressure in 0.25 to 1 and each velocity component in -1.5 to 1.5, independently from cell to cell.
All inputs are finite; a program needn't handle non-finite values.
Results may differ from the reference program's by a relative error of at most 0.00035.
Values sent between devices are 32-bit elements; how exact they have to be, the bound alone decides.
No kernel may reach another device: no remote copies, remote signals or barrier semaphores. Data moves between devices by JAX's collectives and lax.ppermute only.
A program may use at most 64 MiB of HBM per device.

```python
import math
import jax
import jax.numpy as jnp
from jax import lax

NX = 32
NY = 1024
NZ = 512


def draw_fields(key, part):
    key = jax.random.fold_in(key, 11)
    first, second, third = jax.random.split(key, 3)
    density = jnp.exp(jax.random.uniform(first, (NX, NZ, NY), jnp.float32, -math.log(2.0), math.log(2.0)))
    velocity = jnp.clip(0.75 * jax.random.normal(second, (3, NX, NZ, NY), jnp.float32), -1.5, 1.5)
    pressure = jnp.exp(jax.random.uniform(third, (NX, NZ, NY), jnp.float32, -math.log(4.0), 0.0))
    return jnp.concatenate([density[None], velocity, pressure[None]], 0).astype(jnp.float32)


def setup_inputs(seed: int = 0) -> dict:
    keys = jax.random.split(jax.random.key(seed), 2)
    return {
        "fields": draw_fields(jax.random.fold_in(keys[1], 71), 0),
    }


adiabatic = 1.4
time_ratio = 0.03
shock_factor = (adiabatic + 1.0) / (2.0 * adiabatic)
floor_share = 0.1

def take_slice(values, start, stop, direction):
    return lax.slice_in_dim(values, start, stop, axis=direction)

def periodic(values, direction):
    length = values.shape[direction]
    return jnp.concatenate([take_slice(values, length - 3, length, direction), values, take_slice(values, 0, 3, direction)], direction)

def reconstruct(padded, direction):
    length = padded.shape[direction]
    near_left = take_slice(padded, 1, length - 2, direction)
    near_right = take_slice(padded, 2, length - 1, direction)
    interface = 7.0 / 12.0 * (near_left + near_right) - 1.0 / 12.0 * (take_slice(padded, 0, length - 3, direction) + take_slice(padded, 3, length, direction))
    interface = jnp.clip(interface, jnp.minimum(near_left, near_right), jnp.maximum(near_left, near_right))
    centre = take_slice(padded, 2, length - 2, direction)
    below = take_slice(padded, 1, length - 3, direction)
    above = take_slice(padded, 3, length - 1, direction)
    lowest = jnp.minimum(jnp.minimum(below, centre), above)
    highest = jnp.maximum(jnp.maximum(below, centre), above)
    left_edge = take_slice(interface, 0, length - 4, direction)
    right_edge = take_slice(interface, 1, length - 3, direction)
    spread = right_edge - left_edge
    offset = spread * (centre - 0.5 * (left_edge + right_edge))
    ceiling = spread * spread / 6.0
    new_left = jnp.where(offset > ceiling, 3.0 * centre - 2.0 * right_edge, left_edge)
    new_right = jnp.where(offset < -ceiling, 3.0 * centre - 2.0 * left_edge, right_edge)
    new_left = jnp.clip(new_left, lowest, highest)
    new_right = jnp.clip(new_right, lowest, highest)
    cell_count = length - 4
    return (take_slice(new_right, 0, cell_count - 1, direction), take_slice(new_left, 1, cell_count, direction))

def conserved(primitives):
    density = primitives[0]
    velocity = primitives[1:4]
    momentum = density * velocity
    energy = primitives[4] / (adiabatic - 1.0) + 0.5 * lax.optimization_barrier(jnp.sum(momentum * velocity, axis=0))
    return jnp.concatenate([density[None], momentum, energy[None]], 0)

def primitive(totals):
    density = totals[0]
    velocity = totals[1:4] / density
    pressure = (adiabatic - 1.0) * (totals[4] - 0.5 * lax.optimization_barrier(jnp.sum(totals[1:4] * velocity, axis=0)))
    return jnp.concatenate([density[None], velocity, pressure[None]], 0)

def riemann(left_state, right_state, normal):
    dens_left = left_state[0]
    dens_right = right_state[0]
    speed_left = left_state[normal]
    speed_right = right_state[normal]
    press_left = left_state[4]
    press_right = right_state[4]
    sound_left = jnp.sqrt(adiabatic * press_left * dens_left)
    sound_right = jnp.sqrt(adiabatic * press_right * dens_right)
    pressure_floor = floor_share * jnp.minimum(press_left, press_right)
    pressure_star = 0.5 * (press_left + press_right)

    def wave_speeds(guess):
        wave_left = sound_left * jnp.sqrt(1.0 + shock_factor * (guess / press_left - 1.0))
        wave_right = sound_right * jnp.sqrt(1.0 + shock_factor * (guess / press_right - 1.0))
        return (wave_left, wave_right)
    for repeat in range(5):
        wave_left, wave_right = wave_speeds(pressure_star)
        pressure_star = jnp.maximum((wave_right * press_left + wave_left * press_right + wave_left * wave_right * (speed_left - speed_right)) / (wave_left + wave_right), pressure_floor)
    wave_left, wave_right = wave_speeds(pressure_star)
    speed_star = (wave_left * speed_left + wave_right * speed_right + press_left - press_right) / (wave_left + wave_right)
    return (pressure_star, speed_star)

def sweep(padded, direction, normal):
    left_state, right_state = reconstruct(padded, direction)
    pressure_star, speed_star = riemann(left_state, right_state, normal)
    fluxes = jnp.maximum(speed_star, 0.0) * conserved(left_state) + jnp.minimum(speed_star, 0.0) * conserved(right_state)
    fluxes = fluxes.at[normal].add(pressure_star)
    fluxes = fluxes.at[4].add(pressure_star * speed_star)
    length = padded.shape[direction]
    interior = take_slice(padded, 3, length - 3, direction)
    flux_count = length - 5
    totals = conserved(interior) - time_ratio * (take_slice(fluxes, 1, flux_count, direction) - take_slice(fluxes, 0, flux_count - 1, direction))
    return primitive(totals)

def reference(fields):

    def one_plane(plane_fields):
        updated = sweep(periodic(plane_fields, 2), 2, 2)
        return sweep(periodic(updated, 1), 1, 3)
    planes = lax.map(one_plane, jnp.moveaxis(fields, 1, 0))
    return jnp.moveaxis(planes, 0, 1)
```

```python
import jax
import jax.numpy as jnp
from jax import lax
from jax.experimental import pallas as pl
from jax.experimental.pallas import tpu as pltpu
from jax.sharding import PartitionSpec as P

adiabatic = 1.4
time_ratio = 0.03
shock_factor = (adiabatic + 1.0) / (2.0 * adiabatic)
floor_share = 0.1
F32 = jnp.float32
SIDE = 3


def reciprocal(values):
    return pl.reciprocal(values, approx=True)


def edges(cells, count):
    far_left, near_left = cells[: count + 3], cells[1 : count + 4]
    near_right, far_right = cells[2 : count + 5], cells[3:]
    face = (7.0 / 12.0) * (near_left + near_right) - (1.0 / 12.0) * (far_left + far_right)
    face = jnp.maximum(face, jnp.minimum(near_left, near_right))
    face = jnp.minimum(face, jnp.maximum(near_left, near_right))
    centre = cells[2 : count + 4]
    left, right = face[: count + 2], face[1:]
    spread = right - left
    below = centre - left
    above = right - centre
    twice_below = below + below
    twice_above = above + above
    monotone = below * above > 0.0
    new_left = jnp.where(
        spread * (below - twice_above) > 0.0,
        centre - jnp.where(monotone, twice_above, 0.0),
        left,
    )
    new_right = jnp.where(
        spread * (twice_below - above) < 0.0,
        centre + jnp.where(monotone, twice_below, 0.0),
        right,
    )
    return new_right[: count + 1], new_left[1:]


def star(dens_left, speed_left, press_left, dens_right, speed_right, press_right):
    scale = adiabatic * shock_factor
    offset = (1.0 - shock_factor) / shock_factor
    scale_left = scale * dens_left
    scale_right = scale * dens_right
    shift_left = offset * press_left
    shift_right = offset * press_right
    jump = speed_left - speed_right
    floor = floor_share * jnp.minimum(press_left, press_right)
    guess = 0.5 * (press_left + press_right)
    for _ in range(5):
        slow_left = lax.rsqrt(scale_left * (guess + shift_left))
        slow_right = lax.rsqrt(scale_right * (guess + shift_right))
        guess = (press_left * slow_left + press_right * slow_right + jump) * reciprocal(
            slow_left + slow_right
        )
        guess = jnp.maximum(guess, floor)
    slow_left = lax.rsqrt(scale_left * (guess + shift_left))
    slow_right = lax.rsqrt(scale_right * (guess + shift_right))
    speed = (
        slow_right * speed_left
        + slow_left * speed_right
        + (press_left - press_right) * (slow_left * slow_right)
    ) * reciprocal(slow_left + slow_right)
    return guess, speed


def advance(cells, count, normal):
    pairs = [edges(c, count) for c in cells]
    left = [p[0] for p in pairs]
    right = [p[1] for p in pairs]
    press_star, speed_star = star(left[0], left[normal], left[4], right[0], right[normal], right[4])
    upwind = speed_star > 0.0
    state = [jnp.where(upwind, a, b) for a, b in zip(left, right)]
    speed = time_ratio * speed_star
    mass = speed * state[0]
    kinetic = 0.5 * (state[1] * state[1] + state[2] * state[2] + state[3] * state[3])
    fluxes = [mass] + [mass * state[i] for i in (1, 2, 3)]
    fluxes[normal] = fluxes[normal] + time_ratio * press_star
    fluxes.append(
        speed * ((1.0 / (adiabatic - 1.0)) * state[4] + press_star) + mass * kinetic
    )
    mid = [c[3 : count + 3] for c in cells]
    change = [f[1:] - f[:-1] for f in fluxes]
    momentum = [mid[0] * mid[i] for i in (1, 2, 3)]
    energy = (1.0 / (adiabatic - 1.0)) * mid[4] + 0.5 * (
        momentum[0] * mid[1] + momentum[1] * mid[2] + momentum[2] * mid[3]
    )
    density = mid[0] - change[0]
    momentum = [m - c for m, c in zip(momentum, change[1:4])]
    energy = energy - change[4]
    thin = reciprocal(density)
    velocity = [m * thin for m in momentum]
    pressure = (adiabatic - 1.0) * (
        energy
        - 0.5 * (momentum[0] * velocity[0] + momentum[1] * velocity[1] + momentum[2] * velocity[2])
    )
    return [density] + velocity + [pressure]


def to_lines(x_ref, lines_ref):
    for f in range(5):
        for b in range(4):
            turned = x_ref[f, b * 128 : (b + 1) * 128, :].T
            lines_ref[f, b * 64 : (b + 1) * 64, :] = turned[:64]
            lines_ref[f, 256 + b * 64 : 256 + (b + 1) * 64, :] = turned[64:]


def swap_halves(tile):
    return pltpu.roll(tile, 4, 0)


def pack_y(x_ref, first_ref, last_ref, lines_ref):
    to_lines(x_ref, lines_ref)
    for f in range(5):
        for k in range(3):
            first_ref[f, k] = swap_halves(lines_ref[f, pl.ds(k, 8, stride=64), :])
            last_ref[f, k] = swap_halves(lines_ref[f, pl.ds(61 + k, 8, stride=64), :])


Y_CHUNK = 10


def inner_y(x_ref, new_ref, lines_ref, old_ref):
    to_lines(x_ref, lines_ref)
    for f in range(5):
        for k in range(64):
            old_ref[f, k] = lines_ref[f, pl.ds(k, 8, stride=64), :]
    for f in range(5):
        for k in (0, 1, 2, 61, 62, 63):
            new_ref[f, k] = old_ref[f, k]

    def step(i, carry):
        at = jnp.minimum(i * Y_CHUNK, 58 - Y_CHUNK)
        cells = [old_ref[f, pl.ds(at, Y_CHUNK + 6)] for f in range(5)]
        out = advance(cells, Y_CHUNK, 2)
        for f in range(5):
            new_ref[f, pl.ds(at + 3, Y_CHUNK)] = out[f]
        return carry

    lax.fori_loop(0, -(-58 // Y_CHUNK), step, 0)


def outer_y(x_ref, new_ref, before_ref, after_ref, z_ref, first_ref, last_ref, lines_ref, nat_ref):
    to_lines(x_ref, lines_ref)
    low = lax.broadcasted_iota(jnp.int32, (8, 128), 0) < 4
    left, right = [], []
    for f in range(5):
        tile = lambda k: lines_ref[f, pl.ds(k, 8, stride=64), :]
        head = [tile(k) for k in range(6)]
        tail = [tile(58 + k) for k in range(6)]
        before = [jnp.where(low, before_ref[f, k], swap_halves(tail[3 + k])) for k in range(3)]
        after = [jnp.where(low, swap_halves(head[k]), after_ref[f, k]) for k in range(3)]
        left.append(jnp.stack(before + head))
        right.append(jnp.stack(tail + after))
    for cells, base in ((left, 0), (right, 61)):
        out = advance(cells, 3, 2)
        for f in range(5):
            for k in range(3):
                lines_ref[f, pl.ds(base + k, 8, stride=64), :] = out[f][k]
    for f in range(5):
        for k in range(3, 61):
            lines_ref[f, pl.ds(k, 8, stride=64), :] = new_ref[f, k]
        for b in range(4):
            turned = jnp.concatenate(
                [
                    lines_ref[f, b * 64 : (b + 1) * 64, :],
                    lines_ref[f, 256 + b * 64 : 256 + (b + 1) * 64, :],
                ]
            )
            nat_ref[f, b * 128 : (b + 1) * 128, :] = turned.T
    for f in range(5):
        for g in range(4):
            for z in range(16):
                tile = nat_ref[f, pl.ds(128 * g + z, 8, stride=16), :]
                z_ref[f, g, z] = tile
                if z < 3:
                    first_ref[f, g, z] = tile
                if z >= 13:
                    last_ref[f, g, z - 13] = tile


def inner_z(z_ref, new_ref):
    def step(g, carry):
        cells = [z_ref[f, g] for f in range(5)]
        out = advance(cells, 10, 3)
        for f in range(5):
            new_ref[f, g] = out[f]
        return carry

    lax.fori_loop(0, 4, step, 0)


def outer_z(z_ref, new_ref, before_ref, after_ref, out_ref):
    def step(g, carry):
        row = pl.multiple_of(128 * g, 128)
        for f in range(5):
            for z in range(10):
                out_ref[f, pl.ds(row + 3 + z, 8, stride=16), :] = new_ref[f, g, z]
        left = [jnp.concatenate([before_ref[f, g], z_ref[f, g, 0:6]]) for f in range(5)]
        right = [jnp.concatenate([z_ref[f, g, 10:16], after_ref[f, g]]) for f in range(5)]
        for cells, base in ((left, 0), (right, 13)):
            out = advance(cells, 3, 3)
            for f in range(5):
                for z in range(3):
                    out_ref[f, pl.ds(row + base + z, 8, stride=16), :] = out[f][z]
        return carry

    lax.fori_loop(0, 4, step, 0)


def tiles(*shape):
    return jax.ShapeDtypeStruct(shape + (8, 128), F32)


def kernel(body, outs, scratch=(), flops=10**7):
    return pl.pallas_call(
        body,
        out_shape=outs,
        scratch_shapes=[pltpu.VMEM(s, F32) for s in scratch],
        compiler_params=pltpu.CompilerParams(vmem_limit_bytes=24 << 20),
        cost_estimate=pl.CostEstimate(flops=flops, bytes_accessed=1 << 22, transcendentals=flops // 20),
    )


LINES = (5, 512, 128)


def shift(values, axis, by):
    size = lax.axis_size(axis)
    return lax.ppermute(values, axis, [(i, (i + by) % size) for i in range(size)])


def on_device(fields):
    x = fields.reshape(LINES)
    first, last = kernel(pack_y, (tiles(5, 3), tiles(5, 3)), [LINES])(x)
    before = shift(last, "row", 1)
    after = shift(first, "row", -1)
    inner = kernel(inner_y, tiles(5, 64), [LINES, (5, 64, 8, 128)], 10**9)(x)
    state, first, last = kernel(
        outer_y, (tiles(5, 4, 16), tiles(5, 4, 3), tiles(5, 4, 3)), [LINES, LINES]
    )(x, inner, before, after)
    before = shift(last, "col", 1)
    after = shift(first, "col", -1)
    inner = kernel(inner_z, tiles(5, 4, 10), (), 10**9)(state)
    out = kernel(outer_z, jax.ShapeDtypeStruct(LINES, F32))(state, inner, before, after)
    return out.reshape(fields.shape)


def solution(mesh):
    return jax.shard_map(
        on_device,
        mesh=mesh,
        in_specs=(P(None, None, "col", "row"),),
        out_specs=P(None, None, "col", "row"),
        check_vma=False,
    )
```

```python
import jax
import jax.numpy as jnp
from jax import lax
from jax.experimental import pallas as pl
from jax.experimental.pallas import tpu as pltpu
from jax.sharding import PartitionSpec as P

adiabatic = 1.4
time_ratio = 0.03
shock_factor = (adiabatic + 1.0) / (2.0 * adiabatic)
floor_share = 0.1
F32 = jnp.float32
SIDE = 3


def reciprocal(values):
    return pl.reciprocal(values, approx=True)


def edges(cells, count):
    far_left, near_left = cells[: count + 3], cells[1 : count + 4]
    near_right, far_right = cells[2 : count + 5], cells[3:]
    face = (7.0 / 12.0) * (near_left + near_right) - (1.0 / 12.0) * (far_left + far_right)
    face = jnp.maximum(face, jnp.minimum(near_left, near_right))
    face = jnp.minimum(face, jnp.maximum(near_left, near_right))
    centre = cells[2 : count + 4]
    left, right = face[: count + 2], face[1:]
    spread = right - left
    below = centre - left
    above = right - centre
    twice_below = below + below
    twice_above = above + above
    monotone = below * above > 0.0
    new_left = jnp.where(
        spread * (below - twice_above) > 0.0,
        centre - jnp.where(monotone, twice_above, 0.0),
        left,
    )
    new_right = jnp.where(
        spread * (twice_below - above) < 0.0,
        centre + jnp.where(monotone, twice_below, 0.0),
        right,
    )
    return new_right[: count + 1], new_left[1:]


def star(dens_left, speed_left, press_left, dens_right, speed_right, press_right):
    scale = adiabatic * shock_factor
    offset = (1.0 - shock_factor) / shock_factor
    scale_left = scale * dens_left
    scale_right = scale * dens_right
    shift_left = offset * press_left
    shift_right = offset * press_right
    jump = speed_left - speed_right
    floor = floor_share * jnp.minimum(press_left, press_right)
    guess = 0.5 * (press_left + press_right)
    for _ in range(5):
        slow_left = lax.rsqrt(scale_left * (guess + shift_left))
        slow_right = lax.rsqrt(scale_right * (guess + shift_right))
        guess = (press_left * slow_left + press_right * slow_right + jump) * reciprocal(
            slow_left + slow_right
        )
        guess = jnp.maximum(guess, floor)
    slow_left = lax.rsqrt(scale_left * (guess + shift_left))
    slow_right = lax.rsqrt(scale_right * (guess + shift_right))
    speed = (
        slow_right * speed_left
        + slow_left * speed_right
        + (press_left - press_right) * (slow_left * slow_right)
    ) * reciprocal(slow_left + slow_right)
    return guess, speed


def advance(cells, count, normal):
    pairs = [edges(c, count) for c in cells]
    left = [p[0] for p in pairs]
    right = [p[1] for p in pairs]
    press_star, speed_star = star(left[0], left[normal], left[4], right[0], right[normal], right[4])
    upwind = speed_star > 0.0
    state = [jnp.where(upwind, a, b) for a, b in zip(left, right)]
    speed = time_ratio * speed_star
    mass = speed * state[0]
    kinetic = 0.5 * (state[1] * state[1] + state[2] * state[2] + state[3] * state[3])
    fluxes = [mass] + [mass * state[i] for i in (1, 2, 3)]
    fluxes[normal] = fluxes[normal] + time_ratio * press_star
    fluxes.append(
        speed * ((1.0 / (adiabatic - 1.0)) * state[4] + press_star) + mass * kinetic
    )
    mid = [c[3 : count + 3] for c in cells]
    change = [f[1:] - f[:-1] for f in fluxes]
    momentum = [mid[0] * mid[i] for i in (1, 2, 3)]
    energy = (1.0 / (adiabatic - 1.0)) * mid[4] + 0.5 * (
        momentum[0] * mid[1] + momentum[1] * mid[2] + momentum[2] * mid[3]
    )
    density = mid[0] - change[0]
    momentum = [m - c for m, c in zip(momentum, change[1:4])]
    energy = energy - change[4]
    thin = reciprocal(density)
    velocity = [m * thin for m in momentum]
    pressure = (adiabatic - 1.0) * (
        energy
        - 0.5 * (momentum[0] * velocity[0] + momentum[1] * velocity[1] + momentum[2] * velocity[2])
    )
    return [density] + velocity + [pressure]


PITCH = 72
LINES = (5, 8 * PITCH, 128)
ROWS = (5, 512, 128)
HALO = (64, 128)
Y_CHUNK = 15


def tile(lines_ref, f, k):
    return lines_ref[f, pl.ds(k, 8, stride=PITCH), :]


def quarter(f, k):
    return pl.ds(4 * (3 * f + k), 4)


def pack_y(x_ref, lines_ref, near_ref, far_ref, rows_ref, sems):
    copies = [pltpu.make_async_copy(x_ref.at[f], rows_ref.at[f], sems.at[f]) for f in range(5)]
    for copy in copies:
        copy.start()
    for f in range(5):
        copies[f].wait()
        for b in range(4):
            turned = rows_ref[f, b * 128 : (b + 1) * 128, :].T
            lines_ref[f, b * PITCH : b * PITCH + 64, :] = turned[:64]
            lines_ref[f, (4 + b) * PITCH : (4 + b) * PITCH + 64, :] = turned[64:]
    odd = lax.rem(lax.axis_index("row"), 2)
    last = 4 * PITCH + 61
    for ref, base in ((near_ref, (1 - odd) * last), (far_ref, odd * last)):
        for f in range(5):
            for k in range(3):
                ref[quarter(f, k), :] = lines_ref[f, pl.ds(base + k, 4, stride=PITCH), :]
        ref[60:64, :] = jnp.zeros((4, 128), F32)


def inner_y(lines_ref, new_ref):
    def step(i, carry):
        at = jnp.minimum(i * Y_CHUNK, 58 - Y_CHUNK)
        cells = [
            jnp.stack([tile(lines_ref, f, at + k) for k in range(Y_CHUNK + 6)]) for f in range(5)
        ]
        out = advance(cells, Y_CHUNK, 2)
        for f in range(5):
            for k in range(Y_CHUNK):
                new_ref[f, pl.ds(at + 3 + k, 8, stride=PITCH), :] = out[f][k]
        return carry

    lax.fori_loop(0, -(-58 // Y_CHUNK), step, 0)


def outer_y(lines_ref, new_ref, near_ref, far_ref, rows_ref, znear_ref, zfar_ref, ext_ref, done_ref):
    even = lax.rem(lax.axis_index("row"), 2) == 0
    near, far = near_ref[...], far_ref[...]
    before, after = jnp.where(even, far, near), jnp.where(even, near, far)
    for f in range(5):
        for k in range(3):
            q = 4 * (3 * f + k)
            ext_ref[f, k, 0:4, :] = before[q : q + 4]
            ext_ref[f, k, 4:8, :] = lines_ref[f, pl.ds(61 + k, 4, stride=PITCH), :]
            ext_ref[f, 3 + k, 0:4, :] = lines_ref[f, pl.ds(4 * PITCH + k, 4, stride=PITCH), :]
            ext_ref[f, 3 + k, 4:8, :] = after[q : q + 4]
    left = [
        jnp.stack([ext_ref[f, k] for k in range(3)] + [tile(lines_ref, f, k) for k in range(6)])
        for f in range(5)
    ]
    right = [
        jnp.stack(
            [tile(lines_ref, f, 58 + k) for k in range(6)] + [ext_ref[f, 3 + k] for k in range(3)]
        )
        for f in range(5)
    ]
    head = advance(left, 3, 2)
    tail = advance(right, 3, 2)
    for f in range(5):
        for m in range(8):
            done_ref[f, m * 64 : (m + 1) * 64, :] = new_ref[f, m * PITCH : m * PITCH + 64, :]
        for k in range(3):
            done_ref[f, pl.ds(k, 8, stride=64), :] = head[f][k]
            done_ref[f, pl.ds(61 + k, 8, stride=64), :] = tail[f][k]
        for b in range(4):
            turned = jnp.concatenate(
                [
                    done_ref[f, b * 64 : (b + 1) * 64, :],
                    done_ref[f, 256 + b * 64 : 256 + (b + 1) * 64, :],
                ]
            )
            rows_ref[f, b * 128 : (b + 1) * 128, :] = turned.T
    odd = lax.rem(lax.axis_index("col"), 2)
    for f in range(5):
        for g in range(4):
            for z in range(3):
                at = 128 * g + z
                znear_ref[f, g, z] = rows_ref[f, pl.ds(at + 13 * (1 - odd), 8, stride=16), :]
                zfar_ref[f, g, z] = rows_ref[f, pl.ds(at + 13 * odd, 8, stride=16), :]


def line_z(rows_ref, f, row, z):
    return rows_ref[f, pl.ds(row + z, 8, stride=16), :]


def inner_z(rows_ref, new_ref):
    def step(g, carry):
        row = pl.multiple_of(128 * g, 128)
        cells = [jnp.stack([line_z(rows_ref, f, row, z) for z in range(16)]) for f in range(5)]
        out = advance(cells, 10, 3)
        for f in range(5):
            new_ref[f, g] = out[f]
        return carry

    lax.fori_loop(0, 4, step, 0)


def outer_z(rows_ref, new_ref, near_ref, far_ref, out_ref, done_ref, sems):
    even = lax.rem(lax.axis_index("col"), 2) == 0
    copies = []
    for g in range(4):
        row = 128 * g
        left, right = [], []
        for f in range(5):
            near, far = near_ref[f, g], far_ref[f, g]
            before, after = jnp.where(even, far, near), jnp.where(even, near, far)
            left.append(
                jnp.concatenate([before, jnp.stack([line_z(rows_ref, f, row, z) for z in range(6)])])
            )
            right.append(
                jnp.concatenate([jnp.stack([line_z(rows_ref, f, row, 10 + z) for z in range(6)]), after])
            )
            for z in range(10):
                done_ref[f, pl.ds(row + 3 + z, 8, stride=16), :] = new_ref[f, g, z]
        for cells, base in ((left, 0), (right, 13)):
            out = advance(cells, 3, 3)
            for f in range(5):
                for z in range(3):
                    done_ref[f, pl.ds(row + base + z, 8, stride=16), :] = out[f][z]
        copies.append(
            pltpu.make_async_copy(
                done_ref.at[:, pl.ds(row, 128)], out_ref.at[:, pl.ds(row, 128)], sems.at[g]
            )
        )
        copies[g].start()
    for copy in copies:
        copy.wait()


def array(*shape):
    return jax.ShapeDtypeStruct(shape, F32)


def kernel(body, outs, scratch=(), sems=0, flops=10**7, outside=None):
    specs = {}
    if outside == "in":
        specs["in_specs"] = [pl.BlockSpec(memory_space=pl.ANY)]
    if outside == "out":
        specs["out_specs"] = pl.BlockSpec(memory_space=pl.ANY)
    scratch = [pltpu.VMEM(s, F32) for s in scratch]
    if sems:
        scratch.append(pltpu.SemaphoreType.DMA((sems,)))
    return pl.pallas_call(
        body,
        out_shape=outs,
        scratch_shapes=scratch,
        compiler_params=pltpu.CompilerParams(vmem_limit_bytes=24 << 20),
        cost_estimate=pl.CostEstimate(flops=flops, bytes_accessed=1 << 22, transcendentals=flops // 20),
        **specs,
    )


def pairs_near(values, axis):
    size = lax.axis_size(axis)
    return lax.ppermute(values, axis, [(i, i ^ 1) for i in range(size)])


def pairs_far(values, axis):
    size = lax.axis_size(axis)
    return lax.ppermute(values, axis, [(i, (i + 1 if i % 2 else i - 1) % size) for i in range(size)])


def on_device(fields):
    x = fields.reshape(ROWS)
    lines, near, far = kernel(
        pack_y, (array(*LINES), array(*HALO), array(*HALO)), [ROWS], 5, outside="in"
    )(x)
    near = pairs_near(near, "row")
    far = pairs_far(far, "row")
    inner = kernel(inner_y, array(*LINES), flops=10**9)(lines)
    edge = array(5, 4, 3, 8, 128)
    rows, near, far = kernel(
        outer_y, (array(*ROWS), edge, edge), [(5, 6, 8, 128), ROWS]
    )(lines, inner, near, far)
    near = pairs_near(near, "col")
    far = pairs_far(far, "col")
    inner = kernel(inner_z, array(5, 4, 10, 8, 128), flops=10**9)(rows)
    out = kernel(outer_z, array(*ROWS), [ROWS], 4, outside="out")(rows, inner, near, far)
    return out.reshape(fields.shape)


def solution(mesh):
    return jax.shard_map(
        on_device,
        mesh=mesh,
        in_specs=(P(None, None, "col", "row"),),
        out_specs=P(None, None, "col", "row"),
        check_vma=False,
    )
```

```python
import functools

import jax
import jax.numpy as jnp
from jax import lax
from jax.experimental import pallas as pl
from jax.experimental.pallas import tpu as pltpu
from jax.sharding import PartitionSpec as P

adiabatic = 1.4
time_ratio = 0.03
shock_factor = (adiabatic + 1.0) / (2.0 * adiabatic)
floor_share = 0.1
F32 = jnp.float32
SIDE = 3


def reciprocal(values):
    return pl.reciprocal(values, approx=True)


def edges(cells, count):
    far_left, near_left = cells[: count + 3], cells[1 : count + 4]
    near_right, far_right = cells[2 : count + 5], cells[3:]
    face = (7.0 / 12.0) * (near_left + near_right) - (1.0 / 12.0) * (far_left + far_right)
    face = jnp.maximum(face, jnp.minimum(near_left, near_right))
    face = jnp.minimum(face, jnp.maximum(near_left, near_right))
    centre = cells[2 : count + 4]
    left, right = face[: count + 2], face[1:]
    spread = right - left
    below = centre - left
    above = right - centre
    twice_below = below + below
    twice_above = above + above
    monotone = below * above > 0.0
    new_left = jnp.where(
        spread * (below - twice_above) > 0.0,
        centre - jnp.where(monotone, twice_above, 0.0),
        left,
    )
    new_right = jnp.where(
        spread * (twice_below - above) < 0.0,
        centre + jnp.where(monotone, twice_below, 0.0),
        right,
    )
    return new_left, new_right


def star(dens_left, speed_left, press_left, dens_right, speed_right, press_right):
    scale = adiabatic * shock_factor
    offset = (1.0 - shock_factor) / shock_factor
    scale_left = scale * dens_left
    scale_right = scale * dens_right
    shift_left = offset * press_left
    shift_right = offset * press_right
    jump = speed_left - speed_right
    floor = floor_share * jnp.minimum(press_left, press_right)
    guess = 0.5 * (press_left + press_right)
    for _ in range(5):
        slow_left = lax.rsqrt(scale_left * (guess + shift_left))
        slow_right = lax.rsqrt(scale_right * (guess + shift_right))
        guess = (press_left * slow_left + press_right * slow_right + jump) * reciprocal(
            slow_left + slow_right
        )
        guess = jnp.maximum(guess, floor)
    slow_left = lax.rsqrt(scale_left * (guess + shift_left))
    slow_right = lax.rsqrt(scale_right * (guess + shift_right))
    speed = (
        slow_right * speed_left
        + slow_left * speed_right
        + (press_left - press_right) * (slow_left * slow_right)
    ) * reciprocal(slow_left + slow_right)
    return guess, speed


def flux(left, right, normal):
    press_star, speed_star = star(left[0], left[normal], left[4], right[0], right[normal], right[4])
    upwind = speed_star > 0.0
    state = [jnp.where(upwind, a, b) for a, b in zip(left, right)]
    speed = time_ratio * speed_star
    mass = speed * state[0]
    kinetic = 0.5 * (state[1] * state[1] + state[2] * state[2] + state[3] * state[3])
    fluxes = [mass] + [mass * state[i] for i in (1, 2, 3)]
    fluxes[normal] = fluxes[normal] + time_ratio * press_star
    fluxes.append(speed * ((1.0 / (adiabatic - 1.0)) * state[4] + press_star) + mass * kinetic)
    return fluxes


def update(mid, change):
    momentum = [mid[0] * mid[i] for i in (1, 2, 3)]
    energy = (1.0 / (adiabatic - 1.0)) * mid[4] + 0.5 * (
        momentum[0] * mid[1] + momentum[1] * mid[2] + momentum[2] * mid[3]
    )
    density = mid[0] - change[0]
    momentum = [m - c for m, c in zip(momentum, change[1:4])]
    energy = energy - change[4]
    thin = reciprocal(density)
    velocity = [m * thin for m in momentum]
    pressure = (adiabatic - 1.0) * (
        energy
        - 0.5 * (momentum[0] * velocity[0] + momentum[1] * velocity[1] + momentum[2] * velocity[2])
    )
    return [density] + velocity + [pressure]


def inner(cells, count, normal):
    pairs = [edges(c, count) for c in cells]
    left = [p[1][: count + 1] for p in pairs]
    right = [p[0][1:] for p in pairs]
    fluxes = flux(left, right, normal)
    new = update([c[3 : count + 3] for c in cells], [f[1:] - f[:-1] for f in fluxes])
    low = [p[0][0] for p in pairs], [f[0] for f in fluxes]
    high = [p[1][count + 1] for p in pairs], [f[count] for f in fluxes]
    return new, low, high


def outer_low(cells, low, normal):
    pairs = [edges(c, 2) for c in cells]
    left = [p[1][:3] for p in pairs]
    right = [jnp.concatenate([p[0][1:3], edge[None]]) for p, edge in zip(pairs, low[0])]
    fluxes = [jnp.concatenate([a, b[None]]) for a, b in zip(flux(left, right, normal), low[1])]
    return update([c[3:6] for c in cells], [f[1:] - f[:-1] for f in fluxes])


def outer_high(cells, high, normal):
    pairs = [edges(c, 2) for c in cells]
    left = [jnp.concatenate([edge[None], p[1][1:3]]) for p, edge in zip(pairs, high[0])]
    right = [p[0][1:] for p in pairs]
    fluxes = [jnp.concatenate([b[None], a]) for a, b in zip(flux(left, right, normal), high[1])]
    return update([c[2:5] for c in cells], [f[1:] - f[:-1] for f in fluxes])


PITCH = 72
LINES = (5, 8 * PITCH, 128)
ROWS = (5, 512, 128)
HALO = (64, 128)
Y_CHUNK = 29


def tile(lines_ref, f, k):
    return lines_ref[f, pl.ds(k, 8, stride=PITCH), :]


def quarter(f, k):
    return pl.ds(4 * (3 * f + k), 4)


def pack_y(x_ref, lines_ref, near_ref, far_ref, rows_ref, sems):
    copies = [pltpu.make_async_copy(x_ref.at[f], rows_ref.at[f], sems.at[f]) for f in range(5)]
    for copy in copies:
        copy.start()
    odd = lax.rem(lax.axis_index("row"), 2)
    last = 4 * PITCH + 61
    for f in range(5):
        copies[f].wait()
        for b in range(4):
            turned = rows_ref[f, b * 128 : (b + 1) * 128, :].T
            lines_ref[f, b * PITCH : b * PITCH + 64, :] = turned[:64]
            lines_ref[f, (4 + b) * PITCH : (4 + b) * PITCH + 64, :] = turned[64:]
        for ref, base in ((near_ref, (1 - odd) * last), (far_ref, odd * last)):
            for k in range(3):
                ref[quarter(f, k), :] = lines_ref[f, pl.ds(base + k, 4, stride=PITCH), :]
    for ref in (near_ref, far_ref):
        ref[60:64, :] = jnp.zeros((4, 128), F32)


def keep(rim_ref, which, end):
    for i in range(2):
        for f in range(5):
            rim_ref[which, i, f] = end[i][f]


def kept(rim_ref, which):
    return [[rim_ref[which, i, f] for f in range(5)] for i in range(2)]


def inner_y(lines_ref, new_ref, rim_ref):
    for at in range(0, 58, Y_CHUNK):
        cells = [
            jnp.stack([tile(lines_ref, f, at + k) for k in range(Y_CHUNK + 6)]) for f in range(5)
        ]
        new, low, high = inner(cells, Y_CHUNK, 2)
        if at == 0:
            keep(rim_ref, 0, low)
        if at + Y_CHUNK == 58:
            keep(rim_ref, 1, high)
        for f in range(5):
            for k in range(Y_CHUNK):
                new_ref[f, pl.ds(at + 3 + k, 8, stride=PITCH), :] = new[f][k]


def outer_y(lines_ref, new_ref, rim_ref, near_ref, far_ref, rows_ref, znear_ref, zfar_ref, ext_ref, done_ref):
    even = lax.rem(lax.axis_index("row"), 2) == 0
    near, far = near_ref[...], far_ref[...]
    before, after = jnp.where(even, far, near), jnp.where(even, near, far)
    for f in range(5):
        for k in range(3):
            q = 4 * (3 * f + k)
            ext_ref[f, k, 0:4, :] = before[q : q + 4]
            ext_ref[f, k, 4:8, :] = lines_ref[f, pl.ds(61 + k, 4, stride=PITCH), :]
            ext_ref[f, 3 + k, 0:4, :] = lines_ref[f, pl.ds(4 * PITCH + k, 4, stride=PITCH), :]
            ext_ref[f, 3 + k, 4:8, :] = after[q : q + 4]
    below = [
        jnp.stack([ext_ref[f, k] for k in range(3)] + [tile(lines_ref, f, k) for k in range(5)])
        for f in range(5)
    ]
    above = [
        jnp.stack(
            [tile(lines_ref, f, 59 + k) for k in range(5)] + [ext_ref[f, 3 + k] for k in range(3)]
        )
        for f in range(5)
    ]
    head = outer_low(below, kept(rim_ref, 0), 2)
    tail = outer_high(above, kept(rim_ref, 1), 2)
    for f in range(5):
        for m in range(8):
            done_ref[f, m * 64 : (m + 1) * 64, :] = new_ref[f, m * PITCH : m * PITCH + 64, :]
        for k in range(3):
            done_ref[f, pl.ds(k, 8, stride=64), :] = head[f][k]
            done_ref[f, pl.ds(61 + k, 8, stride=64), :] = tail[f][k]
        for b in range(4):
            turned = jnp.concatenate(
                [
                    done_ref[f, b * 64 : (b + 1) * 64, :],
                    done_ref[f, 256 + b * 64 : 256 + (b + 1) * 64, :],
                ]
            )
            rows_ref[f, b * 128 : (b + 1) * 128, :] = turned.T
    odd = lax.rem(lax.axis_index("col"), 2)
    message_z(rows_ref, znear_ref, 13 - 13 * odd)
    message_z(rows_ref, zfar_ref, 13 * odd)


def message_z(rows_ref, message_ref, base):
    for f in range(5):
        for g in range(4):
            for z in range(3):
                message_ref[f, g, z] = rows_ref[f, pl.ds(128 * g + z + base, 8, stride=16), :]


def line_z(rows_ref, f, row, z):
    return rows_ref[f, pl.ds(row + z, 8, stride=16), :]


def inner_z(rows_ref, new_ref, rim_ref, *, start):
    def step(g, carry):
        row = pl.multiple_of(128 * (start + g), 128)
        cells = [jnp.stack([line_z(rows_ref, f, row, z) for z in range(16)]) for f in range(5)]
        new, low, high = inner(cells, 10, 3)
        keep(rim_ref, 2 * g, low)
        keep(rim_ref, 2 * g + 1, high)
        for f in range(5):
            new_ref[f, g] = new[f]
        return carry

    lax.fori_loop(0, 2, step, 0)


def outer_z(rows_ref, one_ref, rim_one_ref, two_ref, rim_two_ref, near_ref, far_ref, out_ref, done_ref, sems):
    even = lax.rem(lax.axis_index("col"), 2) == 0
    copies = []
    for g in range(4):
        row = 128 * g
        new_ref, rim_ref = ((one_ref, rim_one_ref), (two_ref, rim_two_ref))[g // 2]
        h = g % 2
        below, above = [], []
        for f in range(5):
            near, far = near_ref[f, g], far_ref[f, g]
            before, after = jnp.where(even, far, near), jnp.where(even, near, far)
            below.append(
                jnp.concatenate([before, jnp.stack([line_z(rows_ref, f, row, z) for z in range(5)])])
            )
            above.append(
                jnp.concatenate([jnp.stack([line_z(rows_ref, f, row, 11 + z) for z in range(5)]), after])
            )
            for z in range(10):
                done_ref[f, pl.ds(row + 3 + z, 8, stride=16), :] = new_ref[f, h, z]
        head = outer_low(below, kept(rim_ref, 2 * h), 3)
        tail = outer_high(above, kept(rim_ref, 2 * h + 1), 3)
        for cells, base in ((head, 0), (tail, 13)):
            for f in range(5):
                for z in range(3):
                    done_ref[f, pl.ds(row + base + z, 8, stride=16), :] = cells[f][z]
        copies.append(
            pltpu.make_async_copy(
                done_ref.at[:, pl.ds(row, 128)], out_ref.at[:, pl.ds(row, 128)], sems.at[g]
            )
        )
        copies[g].start()
    for copy in copies:
        copy.wait()


def array(*shape):
    return jax.ShapeDtypeStruct(shape, F32)


def kernel(body, outs, scratch=(), sems=0, flops=10**7, outside=None, room=24):
    specs = {}
    if outside == "in":
        specs["in_specs"] = [pl.BlockSpec(memory_space=pltpu.HBM)]
    if outside == "out":
        specs["out_specs"] = pl.BlockSpec(memory_space=pltpu.HBM)
    scratch = [pltpu.VMEM(s, F32) for s in scratch]
    if sems:
        scratch.append(pltpu.SemaphoreType.DMA((sems,)))
    return pl.pallas_call(
        body,
        out_shape=outs,
        scratch_shapes=scratch,
        compiler_params=pltpu.CompilerParams(vmem_limit_bytes=room << 20),
        cost_estimate=pl.CostEstimate(flops=flops, bytes_accessed=1 << 22, transcendentals=flops // 20),
        **specs,
    )


def pairs_near(values, axis):
    size = lax.axis_size(axis)
    return lax.ppermute(values, axis, [(i, i ^ 1) for i in range(size)])


def pairs_far(values, axis):
    size = lax.axis_size(axis)
    return lax.ppermute(values, axis, [(i, (i + 1 if i % 2 else i - 1) % size) for i in range(size)])


def on_device(fields):
    x = pltpu.with_memory_space_constraint(fields.reshape(ROWS), pltpu.HBM)
    lines, near, far = kernel(
        pack_y, (array(*LINES), array(*HALO), array(*HALO)), [ROWS], 5, outside="in"
    )(x)
    near = pairs_near(near, "row")
    far = pairs_far(far, "row")
    new, rim = kernel(inner_y, (array(*LINES), array(2, 2, 5, 8, 128)), flops=10**9)(lines)
    message = array(5, 4, 3, 8, 128)
    rows, near, far = kernel(outer_y, (array(*ROWS), message, message), [(5, 6, 8, 128), ROWS])(
        lines, new, rim, near, far
    )
    far = pairs_far(far, "col")
    half = (array(5, 2, 10, 8, 128), array(4, 2, 5, 8, 128))
    one = kernel(functools.partial(inner_z, start=0), half, flops=10**9)(rows)
    one, rows, near = lax.optimization_barrier((one, rows, near))
    near = pairs_near(near, "col")
    two = kernel(functools.partial(inner_z, start=2), half, flops=10**9)(rows)
    out = kernel(outer_z, array(*ROWS), [ROWS], 4, outside="out")(rows, *one, *two, near, far)
    return out.reshape(fields.shape)


def solution(mesh):
    return jax.shard_map(
        on_device,
        mesh=mesh,
        in_specs=(P(None, None, "col", "row"),),
        out_specs=P(None, None, "col", "row"),
        check_vma=False,
    )
```

```python
import functools

import jax
import jax.numpy as jnp
from jax import lax
from jax.experimental import pallas as pl
from jax.experimental.pallas import tpu as pltpu
from jax.sharding import PartitionSpec as P

adiabatic = 1.4
time_ratio = 0.03
shock_factor = (adiabatic + 1.0) / (2.0 * adiabatic)
floor_share = 0.1
F32 = jnp.float32
SIDE = 3


def reciprocal(values):
    return pl.reciprocal(values, approx=True)


def edges(cells, count):
    far_left, near_left = cells[: count + 3], cells[1 : count + 4]
    near_right, far_right = cells[2 : count + 5], cells[3:]
    face = (7.0 / 12.0) * (near_left + near_right) - (1.0 / 12.0) * (far_left + far_right)
    face = jnp.maximum(face, jnp.minimum(near_left, near_right))
    face = jnp.minimum(face, jnp.maximum(near_left, near_right))
    centre = cells[2 : count + 4]
    left, right = face[: count + 2], face[1:]
    spread = right - left
    below = centre - left
    above = right - centre
    twice_below = below + below
    twice_above = above + above
    monotone = below * above > 0.0
    new_left = jnp.where(
        spread * (below - twice_above) > 0.0,
        centre - jnp.where(monotone, twice_above, 0.0),
        left,
    )
    new_right = jnp.where(
        spread * (twice_below - above) < 0.0,
        centre + jnp.where(monotone, twice_below, 0.0),
        right,
    )
    return new_left, new_right


def star(dens_left, speed_left, press_left, dens_right, speed_right, press_right):
    scale = adiabatic * shock_factor
    offset = (1.0 - shock_factor) / shock_factor
    scale_left = scale * dens_left
    scale_right = scale * dens_right
    shift_left = offset * press_left
    shift_right = offset * press_right
    jump = speed_left - speed_right
    floor = floor_share * jnp.minimum(press_left, press_right)
    guess = 0.5 * (press_left + press_right)
    for _ in range(5):
        slow_left = lax.rsqrt(scale_left * (guess + shift_left))
        slow_right = lax.rsqrt(scale_right * (guess + shift_right))
        guess = (press_left * slow_left + press_right * slow_right + jump) * reciprocal(
            slow_left + slow_right
        )
        guess = jnp.maximum(guess, floor)
    slow_left = lax.rsqrt(scale_left * (guess + shift_left))
    slow_right = lax.rsqrt(scale_right * (guess + shift_right))
    speed = (
        slow_right * speed_left
        + slow_left * speed_right
        + (press_left - press_right) * (slow_left * slow_right)
    ) * reciprocal(slow_left + slow_right)
    return guess, speed


def flux(left, right, normal):
    press_star, speed_star = star(left[0], left[normal], left[4], right[0], right[normal], right[4])
    upwind = speed_star > 0.0
    state = [jnp.where(upwind, a, b) for a, b in zip(left, right)]
    speed = time_ratio * speed_star
    mass = speed * state[0]
    kinetic = 0.5 * (state[1] * state[1] + state[2] * state[2] + state[3] * state[3])
    fluxes = [mass] + [mass * state[i] for i in (1, 2, 3)]
    fluxes[normal] = fluxes[normal] + time_ratio * press_star
    fluxes.append(speed * ((1.0 / (adiabatic - 1.0)) * state[4] + press_star) + mass * kinetic)
    return fluxes


def update(mid, change):
    momentum = [mid[0] * mid[i] for i in (1, 2, 3)]
    energy = (1.0 / (adiabatic - 1.0)) * mid[4] + 0.5 * (
        momentum[0] * mid[1] + momentum[1] * mid[2] + momentum[2] * mid[3]
    )
    density = mid[0] - change[0]
    momentum = [m - c for m, c in zip(momentum, change[1:4])]
    energy = energy - change[4]
    thin = reciprocal(density)
    velocity = [m * thin for m in momentum]
    pressure = (adiabatic - 1.0) * (
        energy
        - 0.5 * (momentum[0] * velocity[0] + momentum[1] * velocity[1] + momentum[2] * velocity[2])
    )
    return [density] + velocity + [pressure]


def inner(cells, count, normal):
    pairs = [edges(c, count) for c in cells]
    left = [p[1][: count + 1] for p in pairs]
    right = [p[0][1:] for p in pairs]
    fluxes = flux(left, right, normal)
    new = update([c[3 : count + 3] for c in cells], [f[1:] - f[:-1] for f in fluxes])
    low = [p[0][0] for p in pairs], [f[0] for f in fluxes]
    high = [p[1][count + 1] for p in pairs], [f[count] for f in fluxes]
    return new, low, high


def outer_low(cells, low, normal):
    pairs = [edges(c, 2) for c in cells]
    left = [p[1][:3] for p in pairs]
    right = [jnp.concatenate([p[0][1:3], edge[None]]) for p, edge in zip(pairs, low[0])]
    fluxes = [jnp.concatenate([a, b[None]]) for a, b in zip(flux(left, right, normal), low[1])]
    return update([c[3:6] for c in cells], [f[1:] - f[:-1] for f in fluxes])


def outer_high(cells, high, normal):
    pairs = [edges(c, 2) for c in cells]
    left = [jnp.concatenate([edge[None], p[1][1:3]]) for p, edge in zip(pairs, high[0])]
    right = [p[0][1:] for p in pairs]
    fluxes = [jnp.concatenate([b[None], a]) for a, b in zip(flux(left, right, normal), high[1])]
    return update([c[2:5] for c in cells], [f[1:] - f[:-1] for f in fluxes])


PAD = 61
PITCH = 72
LINES = (5, 8 * PITCH, 128)
ROWS = (5, 512, 128)
HALO = (64, 128)
Y_CHUNK = 29


def tile(lines_ref, f, k):
    return lines_ref[f, pl.ds(k, 8, stride=PITCH), :]


def quarter(f, k):
    return pl.ds(4 * (3 * f + k), 4)


def pack_y(x_ref, lines_ref, near_ref, far_ref, again_ref, rows_ref, sems):
    copies = [pltpu.make_async_copy(x_ref.at[f], rows_ref.at[f], sems.at[f]) for f in range(5)]
    for copy in copies:
        copy.start()
    odd = lax.rem(lax.axis_index("row"), 2)
    last = 4 * PITCH + 61
    for f in range(5):
        copies[f].wait()
        for b in range(4):
            turned = rows_ref[f, b * 128 : (b + 1) * 128, :].T
            lines_ref[f, b * PITCH : b * PITCH + 64, :] = turned[:64]
            lines_ref[f, (4 + b) * PITCH : (4 + b) * PITCH + 64, :] = turned[64:]
        for ref, base in ((near_ref, (1 - odd) * last), (far_ref, odd * last), (again_ref, (1 - odd) * last)):
            for k in range(3):
                ref[quarter(f, k), :] = lines_ref[f, pl.ds(base + k, 4, stride=PITCH), :]
    for ref in (near_ref, far_ref, again_ref):
        ref[60:64, :] = jnp.zeros((4, 128), F32)


def keep(rim_ref, which, end):
    for i in range(2):
        for f in range(5):
            rim_ref[which, i, f] = end[i][f]


def kept(rim_ref, which):
    return [[rim_ref[which, i, f] for f in range(5)] for i in range(2)]


def inner_y(lines_ref, new_ref, rim_ref):
    for at in range(0, 58, Y_CHUNK):
        cells = [
            jnp.stack([tile(lines_ref, f, at + k) for k in range(Y_CHUNK + 6)]) for f in range(5)
        ]
        new, low, high = inner(cells, Y_CHUNK, 2)
        if at == 0:
            keep(rim_ref, 0, low)
        if at + Y_CHUNK == 58:
            keep(rim_ref, 1, high)
        for f in range(5):
            for k in range(Y_CHUNK):
                new_ref[f, pl.ds(at + 3 + k, 8, stride=PITCH), :] = new[f][k]


def outer_y(lines_ref, new_ref, rim_ref, first_ref, far_ref, second_ref, rows_ref, znear_ref, zfar_ref, ext_ref, rim_rows_ref):
    even = lax.rem(lax.axis_index("row"), 2) == 0
    near = jnp.where(lax.axis_index("row") < 4, first_ref[...], second_ref[...])
    far = far_ref[...]
    before, after = jnp.where(even, far, near), jnp.where(even, near, far)
    for f in range(5):
        for k in range(3):
            q = 4 * (3 * f + k)
            ext_ref[f, k, 0:4, :] = before[q : q + 4]
            ext_ref[f, k, 4:8, :] = lines_ref[f, pl.ds(61 + k, 4, stride=PITCH), :]
            ext_ref[f, 3 + k, 0:4, :] = lines_ref[f, pl.ds(4 * PITCH + k, 4, stride=PITCH), :]
            ext_ref[f, 3 + k, 4:8, :] = after[q : q + 4]
    below = [
        jnp.stack([ext_ref[f, k] for k in range(3)] + [tile(lines_ref, f, k) for k in range(5)])
        for f in range(5)
    ]
    above = [
        jnp.stack(
            [tile(lines_ref, f, 59 + k) for k in range(5)] + [ext_ref[f, 3 + k] for k in range(3)]
        )
        for f in range(5)
    ]
    head = outer_low(below, kept(rim_ref, 0), 2)
    tail = outer_high(above, kept(rim_ref, 1), 2)
    row = lax.broadcasted_iota(jnp.int32, (8, 128), 0)
    for f in range(5):
        for k in range(3):
            rim_rows_ref[f, pl.ds(k, 8, stride=16), :] = head[f][k]
            rim_rows_ref[f, pl.ds(13 + k, 8, stride=16), :] = tail[f][k]
        runs = []
        for m in range(8):
            at = m * PITCH
            first = jnp.where(row < 3, rim_rows_ref[f, 16 * m : 16 * m + 8, :], new_ref[f, at : at + 8, :])
            last = jnp.where(
                row < 5, new_ref[f, at + 56 : at + 64, :], rim_rows_ref[f, 16 * m + 8 : 16 * m + 16, :]
            )
            runs.append([first, new_ref[f, at + 8 : at + 56, :], last])
        for b in range(4):
            turned = jnp.concatenate(runs[b] + runs[4 + b])
            rows_ref[f, b * 128 : (b + 1) * 128, :] = turned.T
    odd = lax.rem(lax.axis_index("col"), 2)
    message_z(rows_ref, znear_ref, 13 - 13 * odd)
    message_z(rows_ref, zfar_ref, 13 * odd)


def message_z(rows_ref, message_ref, base):
    for f in range(5):
        for g in range(4):
            for z in range(3):
                message_ref[(4 * f + g) * 3 + z] = rows_ref[f, pl.ds(128 * g + z + base, 8, stride=16), :]


def line_z(rows_ref, f, row, z):
    return rows_ref[f, pl.ds(row + z, 8, stride=16), :]


def inner_z(rows_ref, new_ref, rim_ref):
    def step(g, carry):
        row = pl.multiple_of(128 * g, 128)
        cells = [jnp.stack([line_z(rows_ref, f, row, z) for z in range(16)]) for f in range(5)]
        new, low, high = inner(cells, 10, 3)
        keep(rim_ref, 2 * g, low)
        keep(rim_ref, 2 * g + 1, high)
        for f in range(5):
            new_ref[f, g] = new[f]
        return carry

    lax.fori_loop(0, 4, step, 0)


def finish(side, rows_ref, new_ref, rim_ref, halo_ref, out_ref, half_ref, sems):
    flat_ref, blocks_ref = half_ref, half_ref.reshape(5, 32, 8, 128)
    copies = []
    for g in range(4):
        row = 128 * g
        cells = []
        for f in range(5):
            own = jnp.stack([line_z(rows_ref, f, row, (0, 11)[side] + z) for z in range(5)])
            pair = (halo_ref[pl.ds((4 * f + g) * 3, 3)], own) if side == 0 else (own, halo_ref[pl.ds((4 * f + g) * 3, 3)])
            cells.append(jnp.concatenate(pair))
        edge = (outer_low, outer_high)[side](cells, kept(rim_ref, 2 * g + side), 3)
        for f in range(5):
            for z in range(3):
                flat_ref[f, pl.ds(64 * g + (0, 5)[side] + z, 8, stride=8), :] = edge[f][z]
            for z in range(5):
                flat_ref[f, pl.ds(64 * g + (3, 0)[side] + z, 8, stride=8), :] = new_ref[
                    f, g, (0, 5)[side] + z
                ]
        copies.append(
            pltpu.make_async_copy(
                blocks_ref.at[:, pl.ds(8 * g, 8)], out_ref.at[:, pl.ds(8 * g, 8), side], sems.at[g]
            )
        )
        copies[g].start()
    for copy in copies:
        copy.wait()


def either_side(is_low, *refs):
    for side in (0, 1):

        @pl.when(is_low if side == 0 else jnp.logical_not(is_low))
        def _():
            finish(side, *refs)


def near_z(rows_ref, new_ref, rim_ref, halo_ref, out_ref, half_ref, sems):
    either_side(lax.rem(lax.axis_index("col"), 2) == 1, rows_ref, new_ref, rim_ref, halo_ref, out_ref, half_ref, sems)


def far_z(rows_ref, new_ref, rim_ref, halo_ref, part_ref, out_ref, half_ref, sems):
    del part_ref
    either_side(lax.rem(lax.axis_index("col"), 2) == 0, rows_ref, new_ref, rim_ref, halo_ref, out_ref, half_ref, sems)


def array(*shape):
    return jax.ShapeDtypeStruct(shape, F32)


def kernel(body, outs, scratch=(), sems=0, flops=10**7, outside=None, room=24, carried=None, moved=1 << 22):
    specs = {}
    if outside == "in":
        specs["in_specs"] = [pl.BlockSpec(memory_space=pltpu.HBM)]
    if outside == "out":
        specs["out_specs"] = pl.BlockSpec(memory_space=pltpu.HBM)
    if carried is not None:
        vmem, hbm = pl.BlockSpec(memory_space=pltpu.VMEM), pl.BlockSpec(memory_space=pltpu.HBM)
        specs["in_specs"] = [vmem] * carried + [hbm]
        specs["input_output_aliases"] = {carried: 0}
    scratch = [pltpu.VMEM(s, F32) for s in scratch]
    if sems:
        scratch.append(pltpu.SemaphoreType.DMA((sems,)))
    return pl.pallas_call(
        body,
        out_shape=outs,
        scratch_shapes=scratch,
        compiler_params=pltpu.CompilerParams(vmem_limit_bytes=room << 20),
        cost_estimate=pl.CostEstimate(flops=flops, bytes_accessed=moved, transcendentals=flops // 20),
        **specs,
    )


def pairs_near(values, axis):
    size = lax.axis_size(axis)
    return lax.ppermute(values, axis, [(i, i ^ 1) for i in range(size)])


def near_rows(values, start):
    columns = lax.axis_size("col")
    steps = []
    for row in range(8):
        for col in range(columns):
            to = (row ^ 1, col) if start <= row < start + 4 else (row, col ^ 1)
            steps.append((row * columns + col, to[0] * columns + to[1]))
    return lax.ppermute(values, ("row", "col"), steps)


def pairs_far(values, axis):
    size = lax.axis_size(axis)
    return lax.ppermute(values, axis, [(i, (i + 1 if i % 2 else i - 1) % size) for i in range(size)])


def on_device(fields):
    x = pltpu.with_memory_space_constraint(fields.reshape(ROWS), pltpu.HBM)
    lines, near, far, again = kernel(
        pack_y, (array(*LINES), array(*HALO), array(*HALO), array(*HALO)), [ROWS], 5, outside="in"
    )(x)
    first = near_rows(near, 0)
    far = pairs_far(far, "row")
    second = near_rows(again, 4)
    new, rim = kernel(inner_y, (array(*LINES), array(2, 2, 5, 8, 128)), flops=10**9)(lines)
    rows, near, far = kernel(outer_y, (array(*ROWS), array(60, 8, 128), array(PAD, 8, 128)), [(5, 6, 8, 128), (5, 128, 128)])(
        lines, new, rim, first, far, second
    )
    far = pairs_far(far, "col")
    near = pairs_near(near, "col")
    new, rim = kernel(inner_z, (array(5, 4, 10, 8, 128), array(8, 2, 5, 8, 128)), flops=1000000000, moved=4194304)(rows)
    split = array(5, 32, 2, 8, 128)
    half = [(5, 256, 128)]
    part = kernel(near_z, split, half, 4, outside="out", flops=10000000, moved=1048576)(rows, new, rim, near)
    out = kernel(far_z, split, half, 4, outside="out", carried=4)(rows, new, rim, far, part)
    return out.reshape(fields.shape)


def solution(mesh):
    return jax.shard_map(
        on_device,
        mesh=mesh,
        in_specs=(P(None, None, "col", "row"),),
        out_specs=P(None, None, "col", "row"),
        check_vma=False,
    )
```

```python
import functools

import jax
import jax.numpy as jnp
from jax import lax
from jax.experimental import pallas as pl
from jax.experimental.pallas import tpu as pltpu
from jax.sharding import PartitionSpec as P

adiabatic = 1.4
time_ratio = 0.03
shock_factor = (adiabatic + 1.0) / (2.0 * adiabatic)
floor_share = 0.1
F32 = jnp.float32
SIDE = 3


def reciprocal(values):
    return pl.reciprocal(values, approx=True)


def edges(cells, count):
    far_left, near_left = cells[: count + 3], cells[1 : count + 4]
    near_right, far_right = cells[2 : count + 5], cells[3:]
    face = (7.0 / 12.0) * (near_left + near_right) - (1.0 / 12.0) * (far_left + far_right)
    face = jnp.maximum(face, jnp.minimum(near_left, near_right))
    face = jnp.minimum(face, jnp.maximum(near_left, near_right))
    centre = cells[2 : count + 4]
    left, right = face[: count + 2], face[1:]
    spread = right - left
    below = centre - left
    above = right - centre
    twice_below = below + below
    twice_above = above + above
    monotone = below * above > 0.0
    new_left = jnp.where(
        spread * (below - twice_above) > 0.0,
        centre - jnp.where(monotone, twice_above, 0.0),
        left,
    )
    new_right = jnp.where(
        spread * (twice_below - above) < 0.0,
        centre + jnp.where(monotone, twice_below, 0.0),
        right,
    )
    return new_left, new_right


def star(dens_left, speed_left, press_left, dens_right, speed_right, press_right):
    scale = adiabatic * shock_factor
    offset = (1.0 - shock_factor) / shock_factor
    scale_left = scale * dens_left
    scale_right = scale * dens_right
    shift_left = offset * press_left
    shift_right = offset * press_right
    jump = speed_left - speed_right
    floor = floor_share * jnp.minimum(press_left, press_right)
    guess = 0.5 * (press_left + press_right)
    for _ in range(5):
        slow_left = lax.rsqrt(scale_left * (guess + shift_left))
        slow_right = lax.rsqrt(scale_right * (guess + shift_right))
        guess = (press_left * slow_left + press_right * slow_right + jump) * reciprocal(
            slow_left + slow_right
        )
        guess = jnp.maximum(guess, floor)
    slow_left = lax.rsqrt(scale_left * (guess + shift_left))
    slow_right = lax.rsqrt(scale_right * (guess + shift_right))
    speed = (
        slow_right * speed_left
        + slow_left * speed_right
        + (press_left - press_right) * (slow_left * slow_right)
    ) * reciprocal(slow_left + slow_right)
    return guess, speed


def flux(left, right, normal):
    press_star, speed_star = star(left[0], left[normal], left[4], right[0], right[normal], right[4])
    upwind = speed_star > 0.0
    state = [jnp.where(upwind, a, b) for a, b in zip(left, right)]
    speed = time_ratio * speed_star
    mass = speed * state[0]
    kinetic = 0.5 * (state[1] * state[1] + state[2] * state[2] + state[3] * state[3])
    fluxes = [mass] + [mass * state[i] for i in (1, 2, 3)]
    fluxes[normal] = fluxes[normal] + time_ratio * press_star
    fluxes.append(speed * ((1.0 / (adiabatic - 1.0)) * state[4] + press_star) + mass * kinetic)
    return fluxes


def update(mid, change):
    momentum = [mid[0] * mid[i] for i in (1, 2, 3)]
    energy = (1.0 / (adiabatic - 1.0)) * mid[4] + 0.5 * (
        momentum[0] * mid[1] + momentum[1] * mid[2] + momentum[2] * mid[3]
    )
    density = mid[0] - change[0]
    momentum = [m - c for m, c in zip(momentum, change[1:4])]
    energy = energy - change[4]
    thin = reciprocal(density)
    velocity = [m * thin for m in momentum]
    pressure = (adiabatic - 1.0) * (
        energy
        - 0.5 * (momentum[0] * velocity[0] + momentum[1] * velocity[1] + momentum[2] * velocity[2])
    )
    return [density] + velocity + [pressure]


def inner(cells, count, normal):
    pairs = [edges(c, count) for c in cells]
    left = [p[1][: count + 1] for p in pairs]
    right = [p[0][1:] for p in pairs]
    fluxes = flux(left, right, normal)
    new = update([c[3 : count + 3] for c in cells], [f[1:] - f[:-1] for f in fluxes])
    low = [p[0][0] for p in pairs], [f[0] for f in fluxes]
    high = [p[1][count + 1] for p in pairs], [f[count] for f in fluxes]
    return new, low, high


def outer_low(cells, low, normal):
    pairs = [edges(c, 2) for c in cells]
    left = [p[1][:3] for p in pairs]
    right = [jnp.concatenate([p[0][1:3], edge[None]]) for p, edge in zip(pairs, low[0])]
    fluxes = [jnp.concatenate([a, b[None]]) for a, b in zip(flux(left, right, normal), low[1])]
    return update([c[3:6] for c in cells], [f[1:] - f[:-1] for f in fluxes])


def outer_high(cells, high, normal):
    pairs = [edges(c, 2) for c in cells]
    left = [jnp.concatenate([edge[None], p[1][1:3]]) for p, edge in zip(pairs, high[0])]
    right = [p[0][1:] for p in pairs]
    fluxes = [jnp.concatenate([b[None], a]) for a, b in zip(flux(left, right, normal), high[1])]
    return update([c[2:5] for c in cells], [f[1:] - f[:-1] for f in fluxes])


PAD = 61
PITCH = 72
LINES = (5, 8 * PITCH, 128)
ROWS = (5, 512, 128)
HALO = (64, 128)
Y_CHUNK = 29


def tile(lines_ref, f, k):
    return lines_ref[f, pl.ds(k, 8, stride=PITCH), :]


def quarter(f, k):
    return pl.ds(4 * (3 * f + k), 4)


def pack_y(x_ref, lines_ref, near_ref, far_ref, again_ref, rows_ref, sems):
    copies = [pltpu.make_async_copy(x_ref.at[f], rows_ref.at[f], sems.at[f]) for f in range(5)]
    for copy in copies:
        copy.start()
    odd = lax.rem(lax.axis_index("row"), 2)
    last = 4 * PITCH + 61
    for f in range(5):
        copies[f].wait()
        for b in range(4):
            turned = rows_ref[f, b * 128 : (b + 1) * 128, :].T
            lines_ref[f, b * PITCH : b * PITCH + 64, :] = turned[:64]
            lines_ref[f, (4 + b) * PITCH : (4 + b) * PITCH + 64, :] = turned[64:]
        for ref, base in ((near_ref, (1 - odd) * last), (far_ref, odd * last), (again_ref, (1 - odd) * last)):
            for k in range(3):
                ref[quarter(f, k), :] = lines_ref[f, pl.ds(base + k, 4, stride=PITCH), :]
    for ref in (near_ref, far_ref, again_ref):
        ref[60:64, :] = jnp.zeros((4, 128), F32)


def keep(rim_ref, which, end):
    for i in range(2):
        for f in range(5):
            rim_ref[which, i, f] = end[i][f]


def kept(rim_ref, which):
    return [[rim_ref[which, i, f] for f in range(5)] for i in range(2)]


def inner_y(lines_ref, new_ref, rim_ref):
    for at in range(0, 58, Y_CHUNK):
        cells = [
            jnp.stack([tile(lines_ref, f, at + k) for k in range(Y_CHUNK + 6)]) for f in range(5)
        ]
        new, low, high = inner(cells, Y_CHUNK, 2)
        if at == 0:
            keep(rim_ref, 0, low)
        if at + Y_CHUNK == 58:
            keep(rim_ref, 1, high)
        for f in range(5):
            for k in range(Y_CHUNK):
                new_ref[f, pl.ds(at + 3 + k, 8, stride=PITCH), :] = new[f][k]


def outer_y(lines_ref, new_ref, rim_ref, first_ref, far_ref, second_ref, rows_ref, znear_ref, zfar_ref, ext_ref, rim_rows_ref):
    even = lax.rem(lax.axis_index("row"), 2) == 0
    near = jnp.where(lax.axis_index("row") < 4, first_ref[...], second_ref[...])
    far = far_ref[...]
    before, after = jnp.where(even, far, near), jnp.where(even, near, far)
    for f in range(5):
        for k in range(3):
            q = 4 * (3 * f + k)
            ext_ref[f, k, 0:4, :] = before[q : q + 4]
            ext_ref[f, k, 4:8, :] = lines_ref[f, pl.ds(61 + k, 4, stride=PITCH), :]
            ext_ref[f, 3 + k, 0:4, :] = lines_ref[f, pl.ds(4 * PITCH + k, 4, stride=PITCH), :]
            ext_ref[f, 3 + k, 4:8, :] = after[q : q + 4]
    below = [
        jnp.stack([ext_ref[f, k] for k in range(3)] + [tile(lines_ref, f, k) for k in range(5)])
        for f in range(5)
    ]
    above = [
        jnp.stack(
            [tile(lines_ref, f, 59 + k) for k in range(5)] + [ext_ref[f, 3 + k] for k in range(3)]
        )
        for f in range(5)
    ]
    head = outer_low(below, kept(rim_ref, 0), 2)
    tail = outer_high(above, kept(rim_ref, 1), 2)
    row = lax.broadcasted_iota(jnp.int32, (8, 128), 0)
    for f in range(5):
        for k in range(3):
            rim_rows_ref[f, pl.ds(k, 8, stride=16), :] = head[f][k]
            rim_rows_ref[f, pl.ds(13 + k, 8, stride=16), :] = tail[f][k]
        runs = []
        for m in range(8):
            at = m * PITCH
            first = jnp.where(row < 3, rim_rows_ref[f, 16 * m : 16 * m + 8, :], new_ref[f, at : at + 8, :])
            last = jnp.where(
                row < 5, new_ref[f, at + 56 : at + 64, :], rim_rows_ref[f, 16 * m + 8 : 16 * m + 16, :]
            )
            runs.append([first, new_ref[f, at + 8 : at + 56, :], last])
        for b in range(4):
            turned = jnp.concatenate(runs[b] + runs[4 + b])
            rows_ref[f, b * 128 : (b + 1) * 128, :] = turned.T
    odd = lax.rem(lax.axis_index("col"), 2)
    message_z(rows_ref, znear_ref, 13 - 13 * odd)
    message_z(rows_ref, zfar_ref, 13 * odd)


def message_z(rows_ref, message_ref, base):
    for f in range(5):
        for g in range(4):
            for z in range(3):
                message_ref[(4 * f + g) * 3 + z] = rows_ref[f, pl.ds(128 * g + z + base, 8, stride=16), :]


def line_z(rows_ref, f, row, z):
    return rows_ref[f, pl.ds(row + z, 8, stride=16), :]


def inner_z(rows_ref, new_ref, rim_ref, *, odd):
    def step(g, carry):
        row = pl.multiple_of(128 * g, 128)
        cells = [jnp.stack([line_z(rows_ref, f, row, z) for z in range(16)]) for f in range(5)]
        new, low, high = inner(cells, 10, 3)
        keep(rim_ref, 2 * g, low)
        keep(rim_ref, 2 * g + 1, high)
        for f in range(5):
            new_ref[f, g] = new[f]
        return carry

    @pl.when(lax.rem(lax.axis_index("col"), 2) == odd)
    def _():
        lax.fori_loop(0, 4, step, 0)


def finish(side, rows_ref, new_ref, rim_ref, halo_ref, out_ref, half_ref, sems):
    flat_ref, blocks_ref = half_ref, half_ref.reshape(5, 32, 8, 128)
    sides = []
    for g in range(4):
        row = 128 * g
        cells = []
        for f in range(5):
            own = jnp.stack([line_z(rows_ref, f, row, (0, 11)[side] + z) for z in range(5)])
            halo = halo_ref[pl.ds((4 * f + g) * 3, 3)]
            cells.append(jnp.concatenate((halo, own) if side == 0 else (own, halo)))
        sides.append((outer_low, outer_high)[side](cells, kept(rim_ref, 2 * g + side), 3))
    copies = []
    for g in range(4):
        for f in range(5):
            for z in range(3):
                flat_ref[f, pl.ds(64 * g + (0, 5)[side] + z, 8, stride=8), :] = sides[g][f][z]
            for z in range(5):
                flat_ref[f, pl.ds(64 * g + (3, 0)[side] + z, 8, stride=8), :] = new_ref[
                    f, g, (0, 5)[side] + z
                ]
        copies.append(
            pltpu.make_async_copy(
                blocks_ref.at[:, pl.ds(8 * g, 8)], out_ref.at[:, pl.ds(8 * g, 8), side], sems.at[g]
            )
        )
        copies[g].start()
    for copy in copies:
        copy.wait()


def near_z(rows_ref, odd_ref, odd_rim_ref, even_ref, even_rim_ref, halo_ref, *refs):
    odd = lax.rem(lax.axis_index("col"), 2) == 1

    @pl.when(odd)
    def _():
        finish(0, rows_ref, odd_ref, odd_rim_ref, halo_ref, *refs)

    @pl.when(jnp.logical_not(odd))
    def _():
        finish(1, rows_ref, even_ref, even_rim_ref, halo_ref, *refs)


def far_z(rows_ref, odd_ref, odd_rim_ref, even_ref, even_rim_ref, halo_ref, part_ref, *refs):
    del part_ref
    odd = lax.rem(lax.axis_index("col"), 2) == 1

    @pl.when(odd)
    def _():
        finish(1, rows_ref, odd_ref, odd_rim_ref, halo_ref, *refs)

    @pl.when(jnp.logical_not(odd))
    def _():
        finish(0, rows_ref, even_ref, even_rim_ref, halo_ref, *refs)


def array(*shape):
    return jax.ShapeDtypeStruct(shape, F32)


def kernel(body, outs, scratch=(), sems=0, flops=10**7, outside=None, room=24, carried=None, moved=1 << 22):
    specs = {}
    if outside == "in":
        specs["in_specs"] = [pl.BlockSpec(memory_space=pltpu.HBM)]
    if outside == "out":
        specs["out_specs"] = pl.BlockSpec(memory_space=pltpu.HBM)
    if carried is not None:
        vmem, hbm = pl.BlockSpec(memory_space=pltpu.VMEM), pl.BlockSpec(memory_space=pltpu.HBM)
        specs["in_specs"] = [vmem] * carried + [hbm]
        specs["input_output_aliases"] = {carried: 0}
    scratch = [pltpu.VMEM(s, F32) for s in scratch]
    if sems:
        scratch.append(pltpu.SemaphoreType.DMA((sems,)))
    return pl.pallas_call(
        body,
        out_shape=outs,
        scratch_shapes=scratch,
        compiler_params=pltpu.CompilerParams(vmem_limit_bytes=room << 20),
        cost_estimate=pl.CostEstimate(flops=flops, bytes_accessed=moved, transcendentals=flops // 20),
        **specs,
    )


def pairs_near(values, axis):
    size = lax.axis_size(axis)
    return lax.ppermute(values, axis, [(i, i ^ 1) for i in range(size)])


def near_rows(values, start):
    columns = lax.axis_size("col")
    steps = []
    for row in range(8):
        for col in range(columns):
            to = (row ^ 1, col) if start <= row < start + 4 else (row, col ^ 1)
            steps.append((row * columns + col, to[0] * columns + to[1]))
    return lax.ppermute(values, ("row", "col"), steps)


def pairs_far(values, axis):
    size = lax.axis_size(axis)
    return lax.ppermute(values, axis, [(i, (i + 1 if i % 2 else i - 1) % size) for i in range(size)])


def on_device(fields):
    x = pltpu.with_memory_space_constraint(fields.reshape(ROWS), pltpu.HBM)
    lines, near, far, again = kernel(
        pack_y, (array(*LINES), array(*HALO), array(*HALO), array(*HALO)), [ROWS], 5, outside="in"
    )(x)
    first = near_rows(near, 0)
    far = pairs_far(far, "row")
    second = near_rows(again, 4)
    new, rim = kernel(inner_y, (array(*LINES), array(2, 2, 5, 8, 128)), flops=10**9)(lines)
    rows, near, far = kernel(outer_y, (array(*ROWS), array(60, 8, 128), array(PAD, 8, 128)), [(5, 6, 8, 128), (5, 128, 128)])(
        lines, new, rim, first, far, second
    )
    far = pairs_far(far, "col")
    inner_cells = (array(5, 4, 10, 8, 128), array(8, 2, 5, 8, 128))
    odd = kernel(functools.partial(inner_z, odd=1), inner_cells, flops=1000000000, moved=4194304)(rows)
    odd, rows, near = lax.optimization_barrier((odd, rows, near))
    near = pairs_near(near, "col")
    even = kernel(functools.partial(inner_z, odd=0), inner_cells, flops=1000000000, moved=4194304)(rows)
    split = array(5, 32, 2, 8, 128)
    half = [(5, 256, 128)]
    part = kernel(near_z, split, half, 4, outside="out", flops=10000000, moved=1048576)(rows, *odd, *even, near)
    out = kernel(far_z, split, half, 4, outside="out", carried=6)(rows, *odd, *even, far, part)
    return out.reshape(fields.shape)


def solution(mesh):
    return jax.shard_map(
        on_device,
        mesh=mesh,
        in_specs=(P(None, None, "col", "row"),),
        out_specs=P(None, None, "col", "row"),
        check_vma=False,
    )
```

```python
import functools

import jax
import jax.numpy as jnp
from jax import lax
from jax.experimental import pallas as pl
from jax.experimental.pallas import tpu as pltpu
from jax.sharding import PartitionSpec as P

adiabatic = 1.4
time_ratio = 0.03
shock_factor = (adiabatic + 1.0) / (2.0 * adiabatic)
floor_share = 0.1
F32 = jnp.float32
SIDE = 3


def reciprocal(values):
    return pl.reciprocal(values, approx=True)


def edges(cells, count):
    far_left, near_left = cells[: count + 3], cells[1 : count + 4]
    near_right, far_right = cells[2 : count + 5], cells[3:]
    face = (7.0 / 12.0) * (near_left + near_right) - (1.0 / 12.0) * (far_left + far_right)
    face = jnp.maximum(face, jnp.minimum(near_left, near_right))
    face = jnp.minimum(face, jnp.maximum(near_left, near_right))
    centre = cells[2 : count + 4]
    left, right = face[: count + 2], face[1:]
    spread = right - left
    below = centre - left
    above = right - centre
    twice_below = below + below
    twice_above = above + above
    monotone = below * above > 0.0
    new_left = jnp.where(
        spread * (below - twice_above) > 0.0,
        centre - jnp.where(monotone, twice_above, 0.0),
        left,
    )
    new_right = jnp.where(
        spread * (twice_below - above) < 0.0,
        centre + jnp.where(monotone, twice_below, 0.0),
        right,
    )
    return new_left, new_right


def star(dens_left, speed_left, press_left, dens_right, speed_right, press_right):
    scale = adiabatic * shock_factor
    offset = (1.0 - shock_factor) / shock_factor
    scale_left = scale * dens_left
    scale_right = scale * dens_right
    shift_left = offset * press_left
    shift_right = offset * press_right
    jump = speed_left - speed_right
    floor = floor_share * jnp.minimum(press_left, press_right)
    guess = 0.5 * (press_left + press_right)
    for _ in range(5):
        slow_left = lax.rsqrt(scale_left * (guess + shift_left))
        slow_right = lax.rsqrt(scale_right * (guess + shift_right))
        guess = (press_left * slow_left + press_right * slow_right + jump) * reciprocal(
            slow_left + slow_right
        )
        guess = jnp.maximum(guess, floor)
    slow_left = lax.rsqrt(scale_left * (guess + shift_left))
    slow_right = lax.rsqrt(scale_right * (guess + shift_right))
    speed = (
        slow_right * speed_left
        + slow_left * speed_right
        + (press_left - press_right) * (slow_left * slow_right)
    ) * reciprocal(slow_left + slow_right)
    return guess, speed


def flux(left, right, normal):
    press_star, speed_star = star(left[0], left[normal], left[4], right[0], right[normal], right[4])
    upwind = speed_star > 0.0
    state = [jnp.where(upwind, a, b) for a, b in zip(left, right)]
    speed = time_ratio * speed_star
    mass = speed * state[0]
    kinetic = 0.5 * (state[1] * state[1] + state[2] * state[2] + state[3] * state[3])
    fluxes = [mass] + [mass * state[i] for i in (1, 2, 3)]
    fluxes[normal] = fluxes[normal] + time_ratio * press_star
    fluxes.append(speed * ((1.0 / (adiabatic - 1.0)) * state[4] + press_star) + mass * kinetic)
    return fluxes


def update(mid, change):
    momentum = [mid[0] * mid[i] for i in (1, 2, 3)]
    energy = (1.0 / (adiabatic - 1.0)) * mid[4] + 0.5 * (
        momentum[0] * mid[1] + momentum[1] * mid[2] + momentum[2] * mid[3]
    )
    density = mid[0] - change[0]
    momentum = [m - c for m, c in zip(momentum, change[1:4])]
    energy = energy - change[4]
    thin = reciprocal(density)
    velocity = [m * thin for m in momentum]
    pressure = (adiabatic - 1.0) * (
        energy
        - 0.5 * (momentum[0] * velocity[0] + momentum[1] * velocity[1] + momentum[2] * velocity[2])
    )
    return [density] + velocity + [pressure]


def inner(cells, count, normal):
    pairs = [edges(c, count) for c in cells]
    left = [p[1][: count + 1] for p in pairs]
    right = [p[0][1:] for p in pairs]
    fluxes = flux(left, right, normal)
    new = update([c[3 : count + 3] for c in cells], [f[1:] - f[:-1] for f in fluxes])
    low = [p[0][0] for p in pairs], [f[0] for f in fluxes]
    high = [p[1][count + 1] for p in pairs], [f[count] for f in fluxes]
    return new, low, high


def outer_low(cells, low, normal):
    pairs = [edges(c, 2) for c in cells]
    left = [p[1][:3] for p in pairs]
    right = [jnp.concatenate([p[0][1:3], edge[None]]) for p, edge in zip(pairs, low[0])]
    fluxes = [jnp.concatenate([a, b[None]]) for a, b in zip(flux(left, right, normal), low[1])]
    return update([c[3:6] for c in cells], [f[1:] - f[:-1] for f in fluxes])


def outer_high(cells, high, normal):
    pairs = [edges(c, 2) for c in cells]
    left = [jnp.concatenate([edge[None], p[1][1:3]]) for p, edge in zip(pairs, high[0])]
    right = [p[0][1:] for p in pairs]
    fluxes = [jnp.concatenate([b[None], a]) for a, b in zip(flux(left, right, normal), high[1])]
    return update([c[2:5] for c in cells], [f[1:] - f[:-1] for f in fluxes])


PAD = 61
PITCH = 72
LINES = (5, 8 * PITCH, 128)
ROWS = (5, 512, 128)
HALO = (64, 128)
Y_CHUNK = 29


def tile(lines_ref, f, k):
    return lines_ref[f, pl.ds(k, 8, stride=PITCH), :]


def quarter(f, k):
    return pl.ds(4 * (3 * f + k), 4)


def pack_y(x_ref, lines_ref, near_ref, far_ref, again_ref, rows_ref, sems):
    copies = [pltpu.make_async_copy(x_ref.at[f], rows_ref.at[f], sems.at[f]) for f in range(5)]
    for copy in copies:
        copy.start()
    odd = lax.rem(lax.axis_index("row"), 2)
    last = 4 * PITCH + 61
    for f in range(5):
        copies[f].wait()
        for b in range(4):
            turned = rows_ref[f, b * 128 : (b + 1) * 128, :].T
            lines_ref[f, b * PITCH : b * PITCH + 64, :] = turned[:64]
            lines_ref[f, (4 + b) * PITCH : (4 + b) * PITCH + 64, :] = turned[64:]
        for ref, base in ((near_ref, (1 - odd) * last), (far_ref, odd * last), (again_ref, (1 - odd) * last)):
            for k in range(3):
                ref[quarter(f, k), :] = lines_ref[f, pl.ds(base + k, 4, stride=PITCH), :]
    for ref in (near_ref, far_ref, again_ref):
        ref[60:64, :] = jnp.zeros((4, 128), F32)


def keep(rim_ref, which, end):
    for i in range(2):
        for f in range(5):
            rim_ref[which, i, f] = end[i][f]


def kept(rim_ref, which):
    return [[rim_ref[which, i, f] for f in range(5)] for i in range(2)]


def starts_early():
    return (lax.axis_index("row") == 0) & (lax.axis_index("col") < 8) & (lax.rem(lax.axis_index("col"), 2) == 1)


def chunk(lines_ref, at):
    cells = [
        jnp.stack([tile(lines_ref, f, at + k) for k in range(Y_CHUNK + 6)]) for f in range(5)
    ]
    return inner(cells, Y_CHUNK, 2)


def early_y(lines_ref, cells_ref, rim_ref):
    @pl.when(starts_early())
    def _():
        new, low, _ = chunk(lines_ref, 0)
        for i in range(2):
            for f in range(5):
                rim_ref[i, f] = low[i][f]
        for f in range(5):
            cells_ref[f] = new[f]


def inner_y(lines_ref, early_ref, early_rim_ref, new_ref, rim_ref):
    def store(new, at):
        for f in range(5):
            for k in range(Y_CHUNK):
                new_ref[f, pl.ds(at + 3 + k, 8, stride=PITCH), :] = new[f][k]

    early = starts_early()

    @pl.when(early)
    def _():
        store([early_ref[f] for f in range(5)], 0)
        keep(rim_ref, 0, [[early_rim_ref[i, f] for f in range(5)] for i in range(2)])

    @pl.when(jnp.logical_not(early))
    def _():
        new, low, _ = chunk(lines_ref, 0)
        keep(rim_ref, 0, low)
        store(new, 0)

    new, _, high = chunk(lines_ref, Y_CHUNK)
    keep(rim_ref, 1, high)
    store(new, Y_CHUNK)


def outer_y(lines_ref, new_ref, rim_ref, first_ref, far_ref, second_ref, rows_ref, znear_ref, zfar_ref, ext_ref, rim_rows_ref):
    even = lax.rem(lax.axis_index("row"), 2) == 0
    near = jnp.where(lax.axis_index("row") < 4, first_ref[...], second_ref[...])
    far = far_ref[...]
    before, after = jnp.where(even, far, near), jnp.where(even, near, far)
    for f in range(5):
        for k in range(3):
            q = 4 * (3 * f + k)
            ext_ref[f, k, 0:4, :] = before[q : q + 4]
            ext_ref[f, k, 4:8, :] = lines_ref[f, pl.ds(61 + k, 4, stride=PITCH), :]
            ext_ref[f, 3 + k, 0:4, :] = lines_ref[f, pl.ds(4 * PITCH + k, 4, stride=PITCH), :]
            ext_ref[f, 3 + k, 4:8, :] = after[q : q + 4]
    below = [
        jnp.stack([ext_ref[f, k] for k in range(3)] + [tile(lines_ref, f, k) for k in range(5)])
        for f in range(5)
    ]
    above = [
        jnp.stack(
            [tile(lines_ref, f, 59 + k) for k in range(5)] + [ext_ref[f, 3 + k] for k in range(3)]
        )
        for f in range(5)
    ]
    head = outer_low(below, kept(rim_ref, 0), 2)
    tail = outer_high(above, kept(rim_ref, 1), 2)
    row = lax.broadcasted_iota(jnp.int32, (8, 128), 0)
    for f in range(5):
        for k in range(3):
            rim_rows_ref[f, pl.ds(k, 8, stride=16), :] = head[f][k]
            rim_rows_ref[f, pl.ds(13 + k, 8, stride=16), :] = tail[f][k]
        runs = []
        for m in range(8):
            at = m * PITCH
            first = jnp.where(row < 3, rim_rows_ref[f, 16 * m : 16 * m + 8, :], new_ref[f, at : at + 8, :])
            last = jnp.where(
                row < 5, new_ref[f, at + 56 : at + 64, :], rim_rows_ref[f, 16 * m + 8 : 16 * m + 16, :]
            )
            runs.append([first, new_ref[f, at + 8 : at + 56, :], last])
        for b in range(4):
            turned = jnp.concatenate(runs[b] + runs[4 + b])
            rows_ref[f, b * 128 : (b + 1) * 128, :] = turned.T
    odd = lax.rem(lax.axis_index("col"), 2)
    message_z(rows_ref, znear_ref, 13 - 13 * odd)
    message_z(rows_ref, zfar_ref, 13 * odd)
    zfar_ref[PAD - 1] = jnp.zeros((8, 128), F32)


def message_z(rows_ref, message_ref, base):
    for f in range(5):
        for g in range(4):
            for z in range(3):
                message_ref[(4 * f + g) * 3 + z] = rows_ref[f, pl.ds(128 * g + z + base, 8, stride=16), :]


def line_z(rows_ref, f, row, z):
    return rows_ref[f, pl.ds(row + z, 8, stride=16), :]


def inner_z(rows_ref, new_ref, rim_ref, *, odd):
    def step(g, carry):
        row = pl.multiple_of(128 * g, 128)
        cells = [jnp.stack([line_z(rows_ref, f, row, z) for z in range(16)]) for f in range(5)]
        new, low, high = inner(cells, 10, 3)
        keep(rim_ref, 2 * g, low)
        keep(rim_ref, 2 * g + 1, high)
        for f in range(5):
            new_ref[f, g] = new[f]
        return carry

    @pl.when(lax.rem(lax.axis_index("col"), 2) == odd)
    def _():
        lax.fori_loop(0, 4, step, 0)


def half_z(side, rows_ref, new_ref, rim_ref, halo_ref, half_ref):
    sides = []
    for g in range(4):
        row = 128 * g
        cells = []
        for f in range(5):
            own = jnp.stack([line_z(rows_ref, f, row, (0, 11)[side] + z) for z in range(5)])
            halo = halo_ref[pl.ds((4 * f + g) * 3, 3)]
            cells.append(jnp.concatenate((halo, own) if side == 0 else (own, halo)))
        sides.append((outer_low, outer_high)[side](cells, kept(rim_ref, 2 * g + side), 3))
    for g in range(4):
        for f in range(5):
            for z in range(3):
                half_ref[f, pl.ds(64 * g + (0, 5)[side] + z, 8, stride=8), :] = sides[g][f][z]
            for z in range(5):
                half_ref[f, pl.ds(64 * g + (3, 0)[side] + z, 8, stride=8), :] = new_ref[
                    f, g, (0, 5)[side] + z
                ]
        yield g


def near_z(rows_ref, odd_ref, odd_rim_ref, even_ref, even_rim_ref, halo_ref, half_ref):
    odd = lax.rem(lax.axis_index("col"), 2) == 1

    @pl.when(odd)
    def _():
        list(half_z(0, rows_ref, odd_ref, odd_rim_ref, halo_ref, half_ref))

    @pl.when(jnp.logical_not(odd))
    def _():
        list(half_z(1, rows_ref, even_ref, even_rim_ref, halo_ref, half_ref))


def far_z(
    rows_ref, odd_ref, odd_rim_ref, even_ref, even_rim_ref, halo_ref, near_ref, out_ref, half_ref, sems
):
    def work(side, new_ref, rim_ref):
        def send(from_ref, start, size, to, sem):
            copy = pltpu.make_async_copy(
                from_ref.reshape(5, 32, 8, 128).at[:, pl.ds(start, size)],
                out_ref.at[:, pl.ds(start, size), to],
                sems.at[sem],
            )
            copy.start()
            return copy

        copies = [send(near_ref, 0, 32, 1 - side, 4)]
        for g in half_z(side, rows_ref, new_ref, rim_ref, halo_ref, half_ref):
            copies.append(send(half_ref, 8 * g, 8, side, g))
        for copy in copies:
            copy.wait()

    odd = lax.rem(lax.axis_index("col"), 2) == 1

    @pl.when(odd)
    def _():
        work(1, odd_ref, odd_rim_ref)

    @pl.when(jnp.logical_not(odd))
    def _():
        work(0, even_ref, even_rim_ref)


def array(*shape):
    return jax.ShapeDtypeStruct(shape, F32)


def kernel(body, outs, scratch=(), sems=0, flops=10**7, outside=None, room=24, moved=1 << 22):
    specs = {}
    if outside == "in":
        specs["in_specs"] = [pl.BlockSpec(memory_space=pltpu.HBM)]
    if outside == "out":
        specs["out_specs"] = pl.BlockSpec(memory_space=pltpu.HBM)
    scratch = [pltpu.VMEM(s, F32) for s in scratch]
    if sems:
        scratch.append(pltpu.SemaphoreType.DMA((sems,)))
    return pl.pallas_call(
        body,
        out_shape=outs,
        scratch_shapes=scratch,
        compiler_params=pltpu.CompilerParams(vmem_limit_bytes=room << 20),
        cost_estimate=pl.CostEstimate(flops=flops, bytes_accessed=moved, transcendentals=flops // 20),
        **specs,
    )


def pairs_near(values, axis):
    size = lax.axis_size(axis)
    return lax.ppermute(values, axis, [(i, i ^ 1) for i in range(size)])


def near_rows(values, start):
    columns = lax.axis_size("col")
    steps = []
    for row in range(8):
        for col in range(columns):
            to = (row ^ 1, col) if start <= row < start + 4 else (row, col ^ 1)
            steps.append((row * columns + col, to[0] * columns + to[1]))
    return lax.ppermute(values, ("row", "col"), steps)


def pairs_far(values, axis):
    size = lax.axis_size(axis)
    return lax.ppermute(values, axis, [(i, (i + 1 if i % 2 else i - 1) % size) for i in range(size)])


def on_device(fields):
    x = pltpu.with_memory_space_constraint(fields.reshape(ROWS), pltpu.HBM)
    lines, near, far, again = kernel(
        pack_y, (array(*LINES), array(*HALO), array(*HALO), array(*HALO)), [ROWS], 5, outside="in"
    )(x)
    ahead = kernel(early_y, (array(5, Y_CHUNK, 8, 128), array(2, 5, 8, 128)))(lines)
    ahead, lines, near, far, again = lax.optimization_barrier((ahead, lines, near, far, again))
    first = near_rows(near, 0)
    far = pairs_far(far, "row")
    second = near_rows(again, 4)
    new, rim = kernel(inner_y, (array(*LINES), array(2, 2, 5, 8, 128)), flops=10**9)(lines, *ahead)
    rows, near, far = kernel(outer_y, (array(*ROWS), array(60, 8, 128), array(PAD, 8, 128)), [(5, 6, 8, 128), (5, 128, 128)])(
        lines, new, rim, first, far, second
    )
    far = pairs_far(far, "col")
    inner_cells = (array(5, 4, 10, 8, 128), array(8, 2, 5, 8, 128))
    odd = kernel(functools.partial(inner_z, odd=1), inner_cells, flops=1000000000, moved=4194304)(rows)
    odd, rows, near = lax.optimization_barrier((odd, rows, near))
    near = pairs_near(near, "col")
    even = kernel(functools.partial(inner_z, odd=0), inner_cells, flops=1000000000, moved=4194304)(rows)
    half = (5, 256, 128)
    part = kernel(near_z, array(*half))(rows, *odd, *even, near)
    out = kernel(far_z, array(5, 32, 2, 8, 128), [half], 5, outside="out")(rows, *odd, *even, far, part)
    return out.reshape(fields.shape)


def solution(mesh):
    return jax.shard_map(
        on_device,
        mesh=mesh,
        in_specs=(P(None, None, "col", "row"),),
        out_specs=P(None, None, "col", "row"),
        check_vma=False,
    )
```

```python
import functools

import jax
import jax.numpy as jnp
from jax import lax
from jax.experimental import pallas as pl
from jax.experimental.pallas import tpu as pltpu
from jax.sharding import PartitionSpec as P

adiabatic = 1.4
time_ratio = 0.03
shock_factor = (adiabatic + 1.0) / (2.0 * adiabatic)
floor_share = 0.1
F32 = jnp.float32
SIDE = 3


def reciprocal(values):
    return pl.reciprocal(values, approx=True)


def edges(cells, count):
    far_left, near_left = cells[: count + 3], cells[1 : count + 4]
    near_right, far_right = cells[2 : count + 5], cells[3:]
    face = (7.0 / 12.0) * (near_left + near_right) - (1.0 / 12.0) * (far_left + far_right)
    face = jnp.maximum(face, jnp.minimum(near_left, near_right))
    face = jnp.minimum(face, jnp.maximum(near_left, near_right))
    centre = cells[2 : count + 4]
    left, right = face[: count + 2], face[1:]
    spread = right - left
    below = centre - left
    above = right - centre
    twice_below = below + below
    twice_above = above + above
    monotone = below * above > 0.0
    new_left = jnp.where(
        spread * (below - twice_above) > 0.0,
        centre - jnp.where(monotone, twice_above, 0.0),
        left,
    )
    new_right = jnp.where(
        spread * (twice_below - above) < 0.0,
        centre + jnp.where(monotone, twice_below, 0.0),
        right,
    )
    return new_left, new_right


def star(dens_left, speed_left, press_left, dens_right, speed_right, press_right):
    scale = adiabatic * shock_factor
    offset = (1.0 - shock_factor) / shock_factor
    scale_left = scale * dens_left
    scale_right = scale * dens_right
    shift_left = offset * press_left
    shift_right = offset * press_right
    jump = speed_left - speed_right
    floor = floor_share * jnp.minimum(press_left, press_right)
    guess = 0.5 * (press_left + press_right)
    for _ in range(5):
        slow_left = lax.rsqrt(scale_left * (guess + shift_left))
        slow_right = lax.rsqrt(scale_right * (guess + shift_right))
        guess = (press_left * slow_left + press_right * slow_right + jump) * reciprocal(
            slow_left + slow_right
        )
        guess = jnp.maximum(guess, floor)
    slow_left = lax.rsqrt(scale_left * (guess + shift_left))
    slow_right = lax.rsqrt(scale_right * (guess + shift_right))
    speed = (
        slow_right * speed_left
        + slow_left * speed_right
        + (press_left - press_right) * (slow_left * slow_right)
    ) * reciprocal(slow_left + slow_right)
    return guess, speed


def flux(left, right, normal):
    press_star, speed_star = star(left[0], left[normal], left[4], right[0], right[normal], right[4])
    upwind = speed_star > 0.0
    state = [jnp.where(upwind, a, b) for a, b in zip(left, right)]
    speed = time_ratio * speed_star
    mass = speed * state[0]
    kinetic = 0.5 * (state[1] * state[1] + state[2] * state[2] + state[3] * state[3])
    fluxes = [mass] + [mass * state[i] for i in (1, 2, 3)]
    fluxes[normal] = fluxes[normal] + time_ratio * press_star
    fluxes.append(speed * ((1.0 / (adiabatic - 1.0)) * state[4] + press_star) + mass * kinetic)
    return fluxes


def update(mid, change):
    momentum = [mid[0] * mid[i] for i in (1, 2, 3)]
    energy = (1.0 / (adiabatic - 1.0)) * mid[4] + 0.5 * (
        momentum[0] * mid[1] + momentum[1] * mid[2] + momentum[2] * mid[3]
    )
    density = mid[0] - change[0]
    momentum = [m - c for m, c in zip(momentum, change[1:4])]
    energy = energy - change[4]
    thin = reciprocal(density)
    velocity = [m * thin for m in momentum]
    pressure = (adiabatic - 1.0) * (
        energy
        - 0.5 * (momentum[0] * velocity[0] + momentum[1] * velocity[1] + momentum[2] * velocity[2])
    )
    return [density] + velocity + [pressure]


def inner(cells, count, normal):
    pairs = [edges(c, count) for c in cells]
    left = [p[1][: count + 1] for p in pairs]
    right = [p[0][1:] for p in pairs]
    fluxes = flux(left, right, normal)
    new = update([c[3 : count + 3] for c in cells], [f[1:] - f[:-1] for f in fluxes])
    low = [p[0][0] for p in pairs], [f[0] for f in fluxes]
    high = [p[1][count + 1] for p in pairs], [f[count] for f in fluxes]
    return new, low, high


def outer_low(cells, low, normal):
    pairs = [edges(c, 2) for c in cells]
    left = [p[1][:3] for p in pairs]
    right = [jnp.concatenate([p[0][1:3], edge[None]]) for p, edge in zip(pairs, low[0])]
    fluxes = [jnp.concatenate([a, b[None]]) for a, b in zip(flux(left, right, normal), low[1])]
    return update([c[3:6] for c in cells], [f[1:] - f[:-1] for f in fluxes])


def outer_high(cells, high, normal):
    pairs = [edges(c, 2) for c in cells]
    left = [jnp.concatenate([edge[None], p[1][1:3]]) for p, edge in zip(pairs, high[0])]
    right = [p[0][1:] for p in pairs]
    fluxes = [jnp.concatenate([b[None], a]) for a, b in zip(flux(left, right, normal), high[1])]
    return update([c[2:5] for c in cells], [f[1:] - f[:-1] for f in fluxes])


PAD = 61
PITCH = 72
LINES = (5, 8 * PITCH, 128)
ROWS = (5, 512, 128)
HALO = (64, 128)
Y_CHUNK = 29


def tile(lines_ref, f, k):
    return lines_ref[f, pl.ds(k, 8, stride=PITCH), :]


def quarter(f, k):
    return pl.ds(4 * (3 * f + k), 4)


def pack_y(x_ref, lines_ref, near_ref, far_ref, again_ref, rows_ref, sems):
    copies = [pltpu.make_async_copy(x_ref.at[f], rows_ref.at[f], sems.at[f]) for f in range(5)]
    for copy in copies:
        copy.start()
    odd = lax.rem(lax.axis_index("row"), 2)
    last = 4 * PITCH + 61
    for f in range(5):
        copies[f].wait()
        for b in range(4):
            turned = rows_ref[f, b * 128 : (b + 1) * 128, :].T
            lines_ref[f, b * PITCH : b * PITCH + 64, :] = turned[:64]
            lines_ref[f, (4 + b) * PITCH : (4 + b) * PITCH + 64, :] = turned[64:]
        for ref, base in ((near_ref, (1 - odd) * last), (far_ref, odd * last), (again_ref, (1 - odd) * last)):
            for k in range(3):
                ref[quarter(f, k), :] = lines_ref[f, pl.ds(base + k, 4, stride=PITCH), :]
    for ref in (near_ref, far_ref, again_ref):
        ref[60:64, :] = jnp.zeros((4, 128), F32)


def keep(rim_ref, which, end):
    for i in range(2):
        for f in range(5):
            rim_ref[which, i, f] = end[i][f]


def kept(rim_ref, which):
    return [[rim_ref[which, i, f] for f in range(5)] for i in range(2)]


def starts_early():
    return (lax.axis_index("row") == 0) & (lax.rem(lax.axis_index("col"), 2) == 1)


def chunk(lines_ref, at):
    cells = [
        jnp.stack([tile(lines_ref, f, at + k) for k in range(Y_CHUNK + 6)]) for f in range(5)
    ]
    return inner(cells, Y_CHUNK, 2)


def early_y(lines_ref, cells_ref, rim_ref):
    @pl.when(starts_early())
    def _():
        new, low, _ = chunk(lines_ref, 0)
        for i in range(2):
            for f in range(5):
                rim_ref[i, f] = low[i][f]
        for f in range(5):
            cells_ref[f] = new[f]


def inner_y(lines_ref, early_ref, early_rim_ref, new_ref, rim_ref):
    def store(new, at):
        for f in range(5):
            for k in range(Y_CHUNK):
                new_ref[f, pl.ds(at + 3 + k, 8, stride=PITCH), :] = new[f][k]

    early = starts_early()

    @pl.when(early)
    def _():
        store([early_ref[f] for f in range(5)], 0)
        keep(rim_ref, 0, [[early_rim_ref[i, f] for f in range(5)] for i in range(2)])

    @pl.when(jnp.logical_not(early))
    def _():
        new, low, _ = chunk(lines_ref, 0)
        keep(rim_ref, 0, low)
        store(new, 0)

    new, _, high = chunk(lines_ref, Y_CHUNK)
    keep(rim_ref, 1, high)
    store(new, Y_CHUNK)


def outer_y(lines_ref, new_ref, rim_ref, first_ref, far_ref, second_ref, rows_ref, zfar_ref, ext_ref, rim_rows_ref):
    even = lax.rem(lax.axis_index("row"), 2) == 0
    near = jnp.where(lax.axis_index("row") < 4, first_ref[...], second_ref[...])
    far = far_ref[...]
    before, after = jnp.where(even, far, near), jnp.where(even, near, far)
    for f in range(5):
        for k in range(3):
            q = 4 * (3 * f + k)
            ext_ref[f, k, 0:4, :] = before[q : q + 4]
            ext_ref[f, k, 4:8, :] = lines_ref[f, pl.ds(61 + k, 4, stride=PITCH), :]
            ext_ref[f, 3 + k, 0:4, :] = lines_ref[f, pl.ds(4 * PITCH + k, 4, stride=PITCH), :]
            ext_ref[f, 3 + k, 4:8, :] = after[q : q + 4]
    below = [
        jnp.stack([ext_ref[f, k] for k in range(3)] + [tile(lines_ref, f, k) for k in range(5)])
        for f in range(5)
    ]
    above = [
        jnp.stack(
            [tile(lines_ref, f, 59 + k) for k in range(5)] + [ext_ref[f, 3 + k] for k in range(3)]
        )
        for f in range(5)
    ]
    head = outer_low(below, kept(rim_ref, 0), 2)
    tail = outer_high(above, kept(rim_ref, 1), 2)
    row = lax.broadcasted_iota(jnp.int32, (8, 128), 0)
    for f in range(5):
        for k in range(3):
            rim_rows_ref[f, pl.ds(k, 8, stride=16), :] = head[f][k]
            rim_rows_ref[f, pl.ds(13 + k, 8, stride=16), :] = tail[f][k]
        runs = []
        for m in range(8):
            at = m * PITCH
            first = jnp.where(row < 3, rim_rows_ref[f, 16 * m : 16 * m + 8, :], new_ref[f, at : at + 8, :])
            last = jnp.where(
                row < 5, new_ref[f, at + 56 : at + 64, :], rim_rows_ref[f, 16 * m + 8 : 16 * m + 16, :]
            )
            runs.append([first, new_ref[f, at + 8 : at + 56, :], last])
        for b in range(4):
            turned = jnp.concatenate(runs[b] + runs[4 + b])
            rows_ref[f, b * 128 : (b + 1) * 128, :] = turned.T
    odd = lax.rem(lax.axis_index("col"), 2)
    message_z(rows_ref, zfar_ref, 13 * odd)
    zfar_ref[PAD - 1] = jnp.zeros((8, 128), F32)


def message_z(rows_ref, message_ref, base):
    for f in range(5):
        for g in range(4):
            for z in range(3):
                message_ref[(4 * f + g) * 3 + z] = rows_ref[f, pl.ds(128 * g + z + base, 8, stride=16), :]


def line_z(rows_ref, f, row, z):
    return rows_ref[f, pl.ds(row + z, 8, stride=16), :]


def inner_z(rows_ref, new_ref, rim_ref, *near_refs, odd):
    def step(g, carry):
        row = pl.multiple_of(128 * g, 128)
        cells = [jnp.stack([line_z(rows_ref, f, row, z) for z in range(16)]) for f in range(5)]
        new, low, high = inner(cells, 10, 3)
        keep(rim_ref, 2 * g, low)
        keep(rim_ref, 2 * g + 1, high)
        for f in range(5):
            new_ref[f, g] = new[f]
        return carry

    for ref in near_refs:
        message_z(rows_ref, ref, 13 - 13 * lax.rem(lax.axis_index("col"), 2))

    @pl.when(lax.rem(lax.axis_index("col"), 2) == odd)
    def _():
        lax.fori_loop(0, 4, step, 0)


def half_z(side, rows_ref, new_ref, rim_ref, halo_ref, half_ref):
    sides = []
    for g in range(4):
        row = 128 * g
        cells = []
        for f in range(5):
            own = jnp.stack([line_z(rows_ref, f, row, (0, 11)[side] + z) for z in range(5)])
            halo = halo_ref[pl.ds((4 * f + g) * 3, 3)]
            cells.append(jnp.concatenate((halo, own) if side == 0 else (own, halo)))
        sides.append((outer_low, outer_high)[side](cells, kept(rim_ref, 2 * g + side), 3))
    for g in range(4):
        for f in range(5):
            for z in range(3):
                half_ref[f, pl.ds(64 * g + (0, 5)[side] + z, 8, stride=8), :] = sides[g][f][z]
            for z in range(5):
                half_ref[f, pl.ds(64 * g + (3, 0)[side] + z, 8, stride=8), :] = new_ref[
                    f, g, (0, 5)[side] + z
                ]
        yield g


def near_z(rows_ref, odd_ref, odd_rim_ref, even_ref, even_rim_ref, halo_ref, half_ref):
    odd = lax.rem(lax.axis_index("col"), 2) == 1

    @pl.when(odd)
    def _():
        list(half_z(0, rows_ref, odd_ref, odd_rim_ref, halo_ref, half_ref))

    @pl.when(jnp.logical_not(odd))
    def _():
        list(half_z(1, rows_ref, even_ref, even_rim_ref, halo_ref, half_ref))


def far_z(
    rows_ref, odd_ref, odd_rim_ref, even_ref, even_rim_ref, halo_ref, near_ref, out_ref, half_ref, sems
):
    def work(side, new_ref, rim_ref):
        def send(from_ref, start, size, to, sem):
            copy = pltpu.make_async_copy(
                from_ref.reshape(5, 32, 8, 128).at[:, pl.ds(start, size)],
                out_ref.at[:, pl.ds(start, size), to],
                sems.at[sem],
            )
            copy.start()
            return copy

        copies = [send(near_ref, 0, 32, 1 - side, 4)]
        for g in half_z(side, rows_ref, new_ref, rim_ref, halo_ref, half_ref):
            copies.append(send(half_ref, 8 * g, 8, side, g))
        for copy in copies:
            copy.wait()

    odd = lax.rem(lax.axis_index("col"), 2) == 1

    @pl.when(odd)
    def _():
        work(1, odd_ref, odd_rim_ref)

    @pl.when(jnp.logical_not(odd))
    def _():
        work(0, even_ref, even_rim_ref)


def array(*shape):
    return jax.ShapeDtypeStruct(shape, F32)


def kernel(body, outs, scratch=(), sems=0, flops=10**7, outside=None, room=24, moved=1 << 22):
    specs = {}
    if outside == "in":
        specs["in_specs"] = [pl.BlockSpec(memory_space=pltpu.HBM)]
    if outside == "out":
        specs["out_specs"] = pl.BlockSpec(memory_space=pltpu.HBM)
    scratch = [pltpu.VMEM(s, F32) for s in scratch]
    if sems:
        scratch.append(pltpu.SemaphoreType.DMA((sems,)))
    return pl.pallas_call(
        body,
        out_shape=outs,
        scratch_shapes=scratch,
        compiler_params=pltpu.CompilerParams(vmem_limit_bytes=room << 20),
        cost_estimate=pl.CostEstimate(flops=flops, bytes_accessed=moved, transcendentals=flops // 20),
        **specs,
    )


def pairs_near(values, axis):
    size = lax.axis_size(axis)
    return lax.ppermute(values, axis, [(i, i ^ 1) for i in range(size)])


def near_rows(values, start):
    columns = lax.axis_size("col")
    steps = []
    for row in range(8):
        for col in range(columns):
            to = (row ^ 1, col) if start <= row < start + 4 else (row, col ^ 1)
            steps.append((row * columns + col, to[0] * columns + to[1]))
    return lax.ppermute(values, ("row", "col"), steps)


def pairs_far(values, axis):
    size = lax.axis_size(axis)
    return lax.ppermute(values, axis, [(i, (i + 1 if i % 2 else i - 1) % size) for i in range(size)])


def on_device(fields):
    x = pltpu.with_memory_space_constraint(fields.reshape(ROWS), pltpu.HBM)
    lines, near, far, again = kernel(
        pack_y, (array(*LINES), array(*HALO), array(*HALO), array(*HALO)), [ROWS], 5, outside="in"
    )(x)
    ahead = kernel(early_y, (array(5, Y_CHUNK, 8, 128), array(2, 5, 8, 128)))(lines)
    ahead, lines, near, far, again = lax.optimization_barrier((ahead, lines, near, far, again))
    first = near_rows(near, 0)
    far = pairs_far(far, "row")
    second = near_rows(again, 4)
    new, rim = kernel(inner_y, (array(*LINES), array(2, 2, 5, 8, 128)), flops=10**9)(lines, *ahead)
    rows, far = kernel(outer_y, (array(*ROWS), array(PAD, 8, 128)), [(5, 6, 8, 128), (5, 128, 128)])(
        lines, new, rim, first, far, second
    )
    far = pairs_far(far, "col")
    inner_cells = (array(5, 4, 10, 8, 128), array(8, 2, 5, 8, 128))
    *odd, near = kernel(functools.partial(inner_z, odd=1), inner_cells + (array(60, 8, 128),), flops=1000000000, moved=4194304)(rows)
    odd, rows, near = lax.optimization_barrier((odd, rows, near))
    near = pairs_near(near, "col")
    even = kernel(functools.partial(inner_z, odd=0), inner_cells, flops=1000000000, moved=4194304)(rows)
    half = (5, 256, 128)
    part = kernel(near_z, array(*half))(rows, *odd, *even, near)
    out = kernel(far_z, array(5, 32, 2, 8, 128), [half], 5, outside="out")(rows, *odd, *even, far, part)
    return out.reshape(fields.shape)


def solution(mesh):
    return jax.shard_map(
        on_device,
        mesh=mesh,
        in_specs=(P(None, None, "col", "row"),),
        out_specs=P(None, None, "col", "row"),
        check_vma=False,
    )
```

```python
import functools

import jax
import jax.numpy as jnp
from jax import lax
from jax.experimental import pallas as pl
from jax.experimental.pallas import tpu as pltpu
from jax.sharding import PartitionSpec as P

adiabatic = 1.4
time_ratio = 0.03
shock_factor = (adiabatic + 1.0) / (2.0 * adiabatic)
floor_share = 0.1
F32 = jnp.float32
SIDE = 3


def reciprocal(values):
    return pl.reciprocal(values, approx=True)


def edges(cells, count):
    far_left, near_left = cells[: count + 3], cells[1 : count + 4]
    near_right, far_right = cells[2 : count + 5], cells[3:]
    face = (7.0 / 12.0) * (near_left + near_right) - (1.0 / 12.0) * (far_left + far_right)
    face = jnp.maximum(face, jnp.minimum(near_left, near_right))
    face = jnp.minimum(face, jnp.maximum(near_left, near_right))
    centre = cells[2 : count + 4]
    left, right = face[: count + 2], face[1:]
    spread = right - left
    below = centre - left
    above = right - centre
    twice_below = below + below
    twice_above = above + above
    monotone = below * above > 0.0
    new_left = jnp.where(
        spread * (below - twice_above) > 0.0,
        centre - jnp.where(monotone, twice_above, 0.0),
        left,
    )
    new_right = jnp.where(
        spread * (twice_below - above) < 0.0,
        centre + jnp.where(monotone, twice_below, 0.0),
        right,
    )
    return new_left, new_right


def star(dens_left, speed_left, press_left, dens_right, speed_right, press_right):
    scale = adiabatic * shock_factor
    offset = (1.0 - shock_factor) / shock_factor
    scale_left = scale * dens_left
    scale_right = scale * dens_right
    shift_left = offset * press_left
    shift_right = offset * press_right
    jump = speed_left - speed_right
    floor = floor_share * jnp.minimum(press_left, press_right)
    guess = 0.5 * (press_left + press_right)
    for _ in range(5):
        slow_left = lax.rsqrt(scale_left * (guess + shift_left))
        slow_right = lax.rsqrt(scale_right * (guess + shift_right))
        guess = (press_left * slow_left + press_right * slow_right + jump) * reciprocal(
            slow_left + slow_right
        )
        guess = jnp.maximum(guess, floor)
    slow_left = lax.rsqrt(scale_left * (guess + shift_left))
    slow_right = lax.rsqrt(scale_right * (guess + shift_right))
    speed = (
        slow_right * speed_left
        + slow_left * speed_right
        + (press_left - press_right) * (slow_left * slow_right)
    ) * reciprocal(slow_left + slow_right)
    return guess, speed


def flux(left, right, normal):
    press_star, speed_star = star(left[0], left[normal], left[4], right[0], right[normal], right[4])
    upwind = speed_star > 0.0
    state = [jnp.where(upwind, a, b) for a, b in zip(left, right)]
    speed = time_ratio * speed_star
    mass = speed * state[0]
    kinetic = 0.5 * (state[1] * state[1] + state[2] * state[2] + state[3] * state[3])
    fluxes = [mass] + [mass * state[i] for i in (1, 2, 3)]
    fluxes[normal] = fluxes[normal] + time_ratio * press_star
    fluxes.append(speed * ((1.0 / (adiabatic - 1.0)) * state[4] + press_star) + mass * kinetic)
    return fluxes


def update(mid, change):
    momentum = [mid[0] * mid[i] for i in (1, 2, 3)]
    energy = (1.0 / (adiabatic - 1.0)) * mid[4] + 0.5 * (
        momentum[0] * mid[1] + momentum[1] * mid[2] + momentum[2] * mid[3]
    )
    density = mid[0] - change[0]
    momentum = [m - c for m, c in zip(momentum, change[1:4])]
    energy = energy - change[4]
    thin = reciprocal(density)
    velocity = [m * thin for m in momentum]
    pressure = (adiabatic - 1.0) * (
        energy
        - 0.5 * (momentum[0] * velocity[0] + momentum[1] * velocity[1] + momentum[2] * velocity[2])
    )
    return [density] + velocity + [pressure]


def inner(cells, count, normal):
    pairs = [edges(c, count) for c in cells]
    left = [p[1][: count + 1] for p in pairs]
    right = [p[0][1:] for p in pairs]
    fluxes = flux(left, right, normal)
    new = update([c[3 : count + 3] for c in cells], [f[1:] - f[:-1] for f in fluxes])
    low = [p[0][0] for p in pairs], [f[0] for f in fluxes]
    high = [p[1][count + 1] for p in pairs], [f[count] for f in fluxes]
    return new, low, high


def outer_low(cells, low, normal):
    pairs = [edges(c, 2) for c in cells]
    left = [p[1][:3] for p in pairs]
    right = [jnp.concatenate([p[0][1:3], edge[None]]) for p, edge in zip(pairs, low[0])]
    fluxes = [jnp.concatenate([a, b[None]]) for a, b in zip(flux(left, right, normal), low[1])]
    return update([c[3:6] for c in cells], [f[1:] - f[:-1] for f in fluxes])


def outer_high(cells, high, normal):
    pairs = [edges(c, 2) for c in cells]
    left = [jnp.concatenate([edge[None], p[1][1:3]]) for p, edge in zip(pairs, high[0])]
    right = [p[0][1:] for p in pairs]
    fluxes = [jnp.concatenate([b[None], a]) for a, b in zip(flux(left, right, normal), high[1])]
    return update([c[2:5] for c in cells], [f[1:] - f[:-1] for f in fluxes])


PAD = 61
PITCH = 72
LINES = (5, 8 * PITCH, 128)
ROWS = (5, 512, 128)
HALO = (64, 128)
Y_CHUNK = 29


def tile(lines_ref, f, k):
    return lines_ref[f, pl.ds(k, 8, stride=PITCH), :]


def quarter(f, k):
    return pl.ds(4 * (3 * f + k), 4)


def pack_y(x_ref, lines_ref, near_ref, far_ref, again_ref, rows_ref, sems):
    copies = [pltpu.make_async_copy(x_ref.at[f], rows_ref.at[f], sems.at[f]) for f in range(5)]
    for copy in copies:
        copy.start()
    odd = lax.rem(lax.axis_index("row"), 2)
    last = 4 * PITCH + 61
    for f in range(5):
        copies[f].wait()
        for b in range(4):
            turned = rows_ref[f, b * 128 : (b + 1) * 128, :].T
            lines_ref[f, b * PITCH : b * PITCH + 64, :] = turned[:64]
            lines_ref[f, (4 + b) * PITCH : (4 + b) * PITCH + 64, :] = turned[64:]
        for ref, base in ((near_ref, (1 - odd) * last), (far_ref, odd * last), (again_ref, (1 - odd) * last)):
            for k in range(3):
                ref[quarter(f, k), :] = lines_ref[f, pl.ds(base + k, 4, stride=PITCH), :]
    for ref in (near_ref, far_ref, again_ref):
        ref[60:64, :] = jnp.zeros((4, 128), F32)


def keep(rim_ref, which, end):
    for i in range(2):
        for f in range(5):
            rim_ref[which, i, f] = end[i][f]


def kept(rim_ref, which):
    return [[rim_ref[which, i, f] for f in range(5)] for i in range(2)]


EARLY_EVEN = 7


def early_counts():
    row, col = lax.axis_index("row"), lax.axis_index("col")
    odd = lax.rem(col, 2) == 1
    return ((row == 0) & odd, Y_CHUNK), ((row == 0) & (col < 8) & jnp.logical_not(odd), EARLY_EVEN)


def chunk(lines_ref, at, count):
    cells = [jnp.stack([tile(lines_ref, f, at + k) for k in range(count + 6)]) for f in range(5)]
    return inner(cells, count, 2)


def early_y(lines_ref, cells_ref, rim_ref):
    for chosen, count in early_counts():

        @pl.when(chosen)
        def _():
            new, low, _ = chunk(lines_ref, 0, count)
            for i in range(2):
                for f in range(5):
                    rim_ref[i, f] = low[i][f]
            for f in range(5):
                cells_ref[f, 0:count] = new[f]


def inner_y(lines_ref, early_ref, early_rim_ref, new_ref, rim_ref):
    def store(new, at, count):
        for f in range(5):
            for k in range(count):
                new_ref[f, pl.ds(at + 3 + k, 8, stride=PITCH), :] = new[f][k]

    def rest(at):
        while at < 58:
            count = min(Y_CHUNK, 58 - at)
            new, low, high = chunk(lines_ref, at, count)
            if at == 0:
                keep(rim_ref, 0, low)
            if at + count == 58:
                keep(rim_ref, 1, high)
            store(new, at, count)
            at += count

    neither = True
    for chosen, count in early_counts():
        neither = jnp.logical_and(neither, jnp.logical_not(chosen))

        @pl.when(chosen)
        def _():
            store([early_ref[f, 0:count] for f in range(5)], 0, count)
            keep(rim_ref, 0, [[early_rim_ref[i, f] for f in range(5)] for i in range(2)])
            rest(count)

    @pl.when(neither)
    def _():
        rest(0)


def outer_y(lines_ref, new_ref, rim_ref, first_ref, far_ref, second_ref, rows_ref, zfar_ref, ext_ref, rim_rows_ref):
    even = lax.rem(lax.axis_index("row"), 2) == 0
    near = jnp.where(lax.axis_index("row") < 4, first_ref[...], second_ref[...])
    far = far_ref[...]
    before, after = jnp.where(even, far, near), jnp.where(even, near, far)
    for f in range(5):
        for k in range(3):
            q = 4 * (3 * f + k)
            ext_ref[f, k, 0:4, :] = before[q : q + 4]
            ext_ref[f, k, 4:8, :] = lines_ref[f, pl.ds(61 + k, 4, stride=PITCH), :]
            ext_ref[f, 3 + k, 0:4, :] = lines_ref[f, pl.ds(4 * PITCH + k, 4, stride=PITCH), :]
            ext_ref[f, 3 + k, 4:8, :] = after[q : q + 4]
    below = [
        jnp.stack([ext_ref[f, k] for k in range(3)] + [tile(lines_ref, f, k) for k in range(5)])
        for f in range(5)
    ]
    above = [
        jnp.stack(
            [tile(lines_ref, f, 59 + k) for k in range(5)] + [ext_ref[f, 3 + k] for k in range(3)]
        )
        for f in range(5)
    ]
    head = outer_low(below, kept(rim_ref, 0), 2)
    tail = outer_high(above, kept(rim_ref, 1), 2)
    row = lax.broadcasted_iota(jnp.int32, (8, 128), 0)
    for f in range(5):
        for k in range(3):
            rim_rows_ref[f, pl.ds(k, 8, stride=16), :] = head[f][k]
            rim_rows_ref[f, pl.ds(13 + k, 8, stride=16), :] = tail[f][k]
        runs = []
        for m in range(8):
            at = m * PITCH
            first = jnp.where(row < 3, rim_rows_ref[f, 16 * m : 16 * m + 8, :], new_ref[f, at : at + 8, :])
            last = jnp.where(
                row < 5, new_ref[f, at + 56 : at + 64, :], rim_rows_ref[f, 16 * m + 8 : 16 * m + 16, :]
            )
            runs.append([first, new_ref[f, at + 8 : at + 56, :], last])
        for b in range(4):
            turned = jnp.concatenate(runs[b] + runs[4 + b])
            rows_ref[f, b * 128 : (b + 1) * 128, :] = turned.T
    odd = lax.rem(lax.axis_index("col"), 2)
    message_z(rows_ref, zfar_ref, 13 * odd)
    zfar_ref[PAD - 1] = jnp.zeros((8, 128), F32)


def message_z(rows_ref, message_ref, base):
    for f in range(5):
        for g in range(4):
            for z in range(3):
                message_ref[(4 * f + g) * 3 + z] = rows_ref[f, pl.ds(128 * g + z + base, 8, stride=16), :]


def line_z(rows_ref, f, row, z):
    return rows_ref[f, pl.ds(row + z, 8, stride=16), :]


def inner_z(rows_ref, new_ref, rim_ref, *near_refs, odd):
    def step(g, carry):
        row = pl.multiple_of(128 * g, 128)
        cells = [jnp.stack([line_z(rows_ref, f, row, z) for z in range(16)]) for f in range(5)]
        new, low, high = inner(cells, 10, 3)
        keep(rim_ref, 2 * g, low)
        keep(rim_ref, 2 * g + 1, high)
        for f in range(5):
            new_ref[f, g] = new[f]
        return carry

    for ref in near_refs:
        message_z(rows_ref, ref, 13 - 13 * lax.rem(lax.axis_index("col"), 2))

    @pl.when(lax.rem(lax.axis_index("col"), 2) == odd)
    def _():
        lax.fori_loop(0, 4, step, 0)


def half_z(side, rows_ref, new_ref, rim_ref, halo_ref, half_ref):
    sides = []
    for g in range(4):
        row = 128 * g
        cells = []
        for f in range(5):
            own = jnp.stack([line_z(rows_ref, f, row, (0, 11)[side] + z) for z in range(5)])
            halo = halo_ref[pl.ds((4 * f + g) * 3, 3)]
            cells.append(jnp.concatenate((halo, own) if side == 0 else (own, halo)))
        sides.append((outer_low, outer_high)[side](cells, kept(rim_ref, 2 * g + side), 3))
    for g in range(4):
        for f in range(5):
            for z in range(3):
                half_ref[f, pl.ds(64 * g + (0, 5)[side] + z, 8, stride=8), :] = sides[g][f][z]
            for z in range(5):
                half_ref[f, pl.ds(64 * g + (3, 0)[side] + z, 8, stride=8), :] = new_ref[
                    f, g, (0, 5)[side] + z
                ]
        yield g


def near_z(rows_ref, odd_ref, odd_rim_ref, even_ref, even_rim_ref, halo_ref, half_ref):
    odd = lax.rem(lax.axis_index("col"), 2) == 1

    @pl.when(odd)
    def _():
        list(half_z(0, rows_ref, odd_ref, odd_rim_ref, halo_ref, half_ref))

    @pl.when(jnp.logical_not(odd))
    def _():
        list(half_z(1, rows_ref, even_ref, even_rim_ref, halo_ref, half_ref))


def far_z(
    rows_ref, odd_ref, odd_rim_ref, even_ref, even_rim_ref, halo_ref, near_ref, out_ref, half_ref, sems
):
    def work(side, new_ref, rim_ref):
        def send(from_ref, start, size, to, sem):
            copy = pltpu.make_async_copy(
                from_ref.reshape(5, 32, 8, 128).at[:, pl.ds(start, size)],
                out_ref.at[:, pl.ds(start, size), to],
                sems.at[sem],
            )
            copy.start()
            return copy

        copies = [send(near_ref, 0, 32, 1 - side, 4)]
        for g in half_z(side, rows_ref, new_ref, rim_ref, halo_ref, half_ref):
            copies.append(send(half_ref, 8 * g, 8, side, g))
        for copy in copies:
            copy.wait()

    odd = lax.rem(lax.axis_index("col"), 2) == 1

    @pl.when(odd)
    def _():
        work(1, odd_ref, odd_rim_ref)

    @pl.when(jnp.logical_not(odd))
    def _():
        work(0, even_ref, even_rim_ref)


def array(*shape):
    return jax.ShapeDtypeStruct(shape, F32)


def kernel(body, outs, scratch=(), sems=0, flops=10**7, outside=None, room=24, moved=1 << 22):
    specs = {}
    if outside == "in":
        specs["in_specs"] = [pl.BlockSpec(memory_space=pltpu.HBM)]
    if outside == "out":
        specs["out_specs"] = pl.BlockSpec(memory_space=pltpu.HBM)
    scratch = [pltpu.VMEM(s, F32) for s in scratch]
    if sems:
        scratch.append(pltpu.SemaphoreType.DMA((sems,)))
    return pl.pallas_call(
        body,
        out_shape=outs,
        scratch_shapes=scratch,
        compiler_params=pltpu.CompilerParams(vmem_limit_bytes=room << 20),
        cost_estimate=pl.CostEstimate(flops=flops, bytes_accessed=moved, transcendentals=flops // 20),
        **specs,
    )


def pairs_near(values, axis):
    size = lax.axis_size(axis)
    return lax.ppermute(values, axis, [(i, i ^ 1) for i in range(size)])


def near_rows(values, start):
    columns = lax.axis_size("col")
    steps = []
    for row in range(8):
        for col in range(columns):
            to = (row ^ 1, col) if start <= row < start + 4 else (row, col ^ 1)
            steps.append((row * columns + col, to[0] * columns + to[1]))
    return lax.ppermute(values, ("row", "col"), steps)


def pairs_far(values, axis):
    size = lax.axis_size(axis)
    return lax.ppermute(values, axis, [(i, (i + 1 if i % 2 else i - 1) % size) for i in range(size)])


def on_device(fields):
    x = pltpu.with_memory_space_constraint(fields.reshape(ROWS), pltpu.HBM)
    lines, near, far, again = kernel(
        pack_y, (array(*LINES), array(*HALO), array(*HALO), array(*HALO)), [ROWS], 5, outside="in"
    )(x)
    ahead = kernel(early_y, (array(5, Y_CHUNK, 8, 128), array(2, 5, 8, 128)))(lines)
    ahead, lines, near, far, again = lax.optimization_barrier((ahead, lines, near, far, again))
    first = near_rows(near, 0)
    far = pairs_far(far, "row")
    second = near_rows(again, 4)
    new, rim = kernel(inner_y, (array(*LINES), array(2, 2, 5, 8, 128)), flops=10**9)(lines, *ahead)
    rows, far = kernel(outer_y, (array(*ROWS), array(PAD, 8, 128)), [(5, 6, 8, 128), (5, 128, 128)])(
        lines, new, rim, first, far, second
    )
    far = pairs_far(far, "col")
    inner_cells = (array(5, 4, 10, 8, 128), array(8, 2, 5, 8, 128))
    *odd, near = kernel(functools.partial(inner_z, odd=1), inner_cells + (array(60, 8, 128),), flops=1000000000, moved=4194304)(rows)
    odd, rows, near = lax.optimization_barrier((odd, rows, near))
    near = pairs_near(near, "col")
    even = kernel(functools.partial(inner_z, odd=0), inner_cells, flops=1000000000, moved=4194304)(rows)
    half = (5, 256, 128)
    part = kernel(near_z, array(*half))(rows, *odd, *even, near)
    out = kernel(far_z, array(5, 32, 2, 8, 128), [half], 5, outside="out")(rows, *odd, *even, far, part)
    return out.reshape(fields.shape)


def solution(mesh):
    return jax.shard_map(
        on_device,
        mesh=mesh,
        in_specs=(P(None, None, "col", "row"),),
        out_specs=P(None, None, "col", "row"),
        check_vma=False,
    )
```
